256 devices in a mesh: tm: 32 (over x, y, core), space: 8 (over z).
Axes of the slice: x: 4, y: 4, z: 8, core: 2. Of those that a mesh axis runs over, the one named last changes fastest.
Arguments:
- sep_block: float32 [32, 1536, 1536], P('tm', 'space'), may hold values from -1 to 10, as said below
- own_couple: bfloat16 [32, 1536, 1536], P('tm', 'space'), may hold values from -0.1875 to 0.1875
- prev_couple: bfloat16 [32, 1536, 1536], P('tm', 'space'), may hold values from -0.1875 to 0.1875
- inner_diag: float32 [32, 1536], P('tm'), may hold values from 0.5 to 4
Outputs:
- reduced_blocks: float32 [32, 1536, 1536], P('tm', 'space')
- left_links: bfloat16 [32, 1536, 1536], P('tm', 'space')
The draws below stay inside these ranges and needn't reach their ends.
Inputs may be any that keep to these rules, and one draw needn't show every extreme that they name: sep_block is symmetric in its last two dimensions; its diagonal entries lie between 3.5 and 10.
All inputs are finite; a program needn't handle non-finite values.
Results may differ from the reference program's by a relative error of at most 0.0083.
Values may be sent and summed in bfloat16 or wider, within the bound.
A program may use at most 64 MiB of HBM per device.

```python
import math
import jax
import jax.numpy as jnp
from jax import lax

BLOCK = 1536
PARTS_SIZE = 32


def draw_sep_block(key, part):
    noise_key, level_key = jax.random.split(jax.random.fold_in(key, 17))
    full_shape = (PARTS_SIZE, BLOCK, BLOCK)
    noise_field = jnp.clip(jax.random.normal(noise_key, full_shape, jnp.float32), -4.0, 4.0)
    diag_values = jax.random.uniform(level_key, (PARTS_SIZE, BLOCK), jnp.float32, 3.5, 10.0)
    off_diagonal = (noise_field + jnp.swapaxes(noise_field, 1, 2)) * (0.7071 / math.sqrt(BLOCK))
    diagonal_mask = jnp.eye(BLOCK, dtype=bool)
    return jnp.where(diagonal_mask[None, :, :], diag_values[:, :, None], off_diagonal)


def block_scale(rng, dims, pieces, low, top_value):
    def one(axis_at, shards_of):
        draws = jax.random.uniform(jax.random.fold_in(jax.random.fold_in(rng, 6), axis_at), (shards_of,), jnp.float32, low / len(pieces), top_value / len(pieces))
        return jnp.repeat(jnp.exp(draws), dims[axis_at] // shards_of).reshape((-1,) + (1,) * (len(dims) - axis_at - 1))

    gain = one(*pieces[0])
    for cut in pieces[1:]:
        gain = gain * one(*cut)
    return gain


def gaussian(key, dims, deviation, most, shards=(), kind=jnp.bfloat16):
    gain = block_scale(key, dims, shards, -0.22, 0.18) if shards else 1.0
    values = jax.random.normal(key, dims, jnp.float32) * deviation * gain
    return jnp.minimum(jnp.maximum(values, -most), most).astype(kind)


def setup_inputs(seed: int = 0) -> dict:
    streams_of = jax.random.split(jax.random.key(seed), 5)
    return {
        "sep_block": draw_sep_block(jax.random.fold_in(streams_of[4], 71), 0),
        "own_couple": gaussian(streams_of[1], (PARTS_SIZE, BLOCK, BLOCK), (BLOCK * 100 // 169) ** -0.5, 0.1875, ((0, 32), (1, 8))),
        "prev_couple": gaussian(streams_of[2], (PARTS_SIZE, BLOCK, BLOCK), (BLOCK * 100 // 169) ** -0.5, 0.1875, ((0, 32), (1, 8))),
        "inner_diag": jnp.clip(jnp.exp(math.log(4.0) - 2.0794415 * jax.random.uniform(streams_of[3], (PARTS_SIZE, BLOCK), jnp.float32) ** block_scale(streams_of[3], (PARTS_SIZE, BLOCK), ((0, 32),), -0.2, 0.2)), 0.5, 4.0),
    }


def scaled_by(matrix, factors):
    return (matrix.astype(jnp.float32) * factors.astype(jnp.float32)[None, :]).astype(jnp.bfloat16)


def outer_form(left_side, right_side):
    return jnp.dot(left_side, right_side.T, preferred_element_type=jnp.float32)


def local_step(partition_item):
    separator, own_rows, prev_rows, pivot_diag = partition_item
    reciprocal = 1.0 / pivot_diag
    own_scaled = scaled_by(own_rows, reciprocal)
    prev_scaled = scaled_by(prev_rows, reciprocal)
    own_form = outer_form(own_scaled, own_rows)
    prev_form = outer_form(prev_scaled, prev_rows)
    coupling = (-outer_form(prev_scaled, own_rows)).astype(jnp.bfloat16)
    return separator - own_form, prev_form, coupling


def reduce_level(schur, link, distance):
    partitions = schur.shape[0]
    pivot_count = partitions // (2 * distance)
    pivots = (jnp.arange(pivot_count) * (2 * distance) + distance - 1).astype(jnp.int32)

    def eliminate(pivot):
        schur_block = lax.dynamic_index_in_dim(schur, pivot, 0, keepdims=False)
        first_link = lax.dynamic_index_in_dim(link, pivot, 0, keepdims=False)
        later = (pivot + distance).astype(jnp.int32)
        later_link = lax.dynamic_index_in_dim(link, later, 0, keepdims=False)
        pivot_scale = (1.0 / jnp.maximum(jnp.diagonal(schur_block), 1.0)).astype(jnp.bfloat16)
        first_scaled = scaled_by(first_link, pivot_scale)
        second_scaled = scaled_by(later_link.T, pivot_scale)
        left_form = jnp.dot(first_scaled, first_link.T, preferred_element_type=jnp.float32)
        right_form = jnp.dot(second_scaled, later_link, preferred_element_type=jnp.float32)
        fill_link = (-jnp.dot(first_scaled, later_link, preferred_element_type=jnp.float32)).astype(jnp.bfloat16)
        return left_form, right_form, fill_link

    left_forms, right_forms, fill_links = lax.map(eliminate, pivots)
    receivers = (pivots + distance).astype(jnp.int32)
    left_after = jnp.concatenate([left_forms[1:], jnp.zeros_like(left_forms[:1])], axis=0)
    updated = (schur[receivers] - left_after) - right_forms
    schur = schur.at[receivers].set(updated)
    link = link.at[receivers].set(fill_links)
    return schur, link


def reference(sep_block, own_couple, prev_couple, inner_diag):
    partial_schur, prev_forms, link = lax.map(local_step, (sep_block, own_couple, prev_couple, inner_diag))
    link = link.at[0].set(jnp.zeros_like(link[0]))
    incoming = jnp.concatenate([prev_forms[1:], jnp.zeros_like(prev_forms[:1])], axis=0)
    schur = partial_schur - incoming
    schur, link = reduce_level(schur, link, 1)
    schur, link = reduce_level(schur, link, 2)
    return schur, link
```

```python
import functools

import jax
import jax.numpy as jnp
from jax import lax
from jax.experimental import pallas as pl
from jax.experimental.pallas import tpu as pltpu
from jax.sharding import PartitionSpec as P

MESH = pl.DeviceIdType.MESH
OWN, PREV = 0, 1


def kernel(
    ring, parts, sep_hbm, own_hbm, prev_hbm, diag_ref, schur_ref, link_ref,
    sep, pair, scaled, links, links_scaled, fills, fills_scaled, sibling, handed, update,
    update_in, far, far_in, last, last_in, final, final_in,
    edge, edge_in, diags, edge2, edge2_in, diags2,
    load_sem, a_send, a_recv, w_send, w_recv, f_send, f_recv,
    d_send, d_recv, d2_send, d2_recv, e_send, e_recv, m_send, m_recv,
):
    rows, width = sep.shape
    tile = 512
    chunk = 16
    z = lax.axis_index("space")
    t = lax.axis_index("tm")
    odd = lax.rem(t, 2)
    role = lax.rem(t, 4)
    is_odd = odd == 1
    inner = jnp.logical_or(role == 1, role == 2)
    sib = t + 1 - 2 * odd
    across = lax.rem(t + 2 * odd - 1 + parts, parts)
    before = lax.rem(t + parts - 1, parts)
    before2 = lax.rem(t + parts - 2, parts)
    after = lax.rem(t + 1, parts)
    after2 = lax.rem(t + 2, parts)

    barrier = pltpu.get_barrier_semaphore()
    for k in range(1, ring):
        pl.semaphore_signal(
            barrier, inc=1, device_id={"space": lax.rem(z + k, ring)}, device_id_type=MESH
        )
    for peer in (before, before2, after, after2):
        pl.semaphore_signal(barrier, inc=1, device_id={"tm": peer}, device_id_type=MESH)

    def mine(step):
        return pl.ds(pl.multiple_of(step * rows, rows), rows)

    loads = [
        pltpu.make_async_copy(own_hbm, pair.at[OWN, mine(z)], load_sem.at[0]),
        pltpu.make_async_copy(prev_hbm, pair.at[PREV, mine(z)], load_sem.at[1]),
        pltpu.make_async_copy(sep_hbm, sep, load_sem.at[2]),
    ]
    for load in loads:
        load.start()
    for load in loads:
        load.wait()
    pl.semaphore_wait(barrier, ring + 3)

    def hop(buf, offset, count, way, step, send_sem, recv_sem):
        slot = lax.rem(z - way * (step - 1) + 2 * ring, ring)
        piece = buf.at[pl.ds(pl.multiple_of(slot * rows + offset, chunk), count)]
        return pltpu.make_async_remote_copy(
            src_ref=piece, dst_ref=piece, send_sem=send_sem, recv_sem=recv_sem,
            device_id={"space": lax.rem(z + way + ring, ring)}, device_id_type=MESH,
        )

    class Ring:
        def __init__(self, streams, send_sem, recv_sem):
            self.streams = streams
            self.sems = send_sem, recv_sem

        def at(self, s, step):
            buf, offset, count, way, _ = self.streams[s]
            at = s * (ring // 2) + step - 1
            return hop(buf, offset, count, way, step, self.sems[0].at[at], self.sems[1].at[at])

        def start(self):
            for s in range(len(self.streams)):
                self.at(s, 1).start()

        def run(self):
            for step in range(1, ring // 2 + 1):
                for s, stream in enumerate(self.streams):
                    if step <= stream[4]:
                        self.at(s, step).wait_recv()
                        if step < stream[4]:
                            self.at(s, step + 1).start()

        def drain(self):
            for s, stream in enumerate(self.streams):
                for step in range(1, stream[4] + 1):
                    self.at(s, step).wait_send()

    far_way, near_way = ring // 2, ring // 2 - 1

    def both_ways(buf):
        half = rows // 2
        return [
            (buf, 0, half, 1, far_way),
            (buf, 0, half, -1, near_way),
            (buf, half, half, -1, far_way),
            (buf, half, half, 1, near_way),
        ]

    ring_a = Ring(
        [
            (pair.at[OWN], 0, rows, 1, far_way),
            (pair.at[PREV], 0, rows, -1, far_way),
            (pair.at[OWN], 0, rows, -1, near_way),
            (pair.at[PREV], 0, rows, 1, near_way),
        ],
        a_send, a_recv,
    )
    ring_w = Ring(both_ways(links), w_send, w_recv)
    ring_f = Ring(both_ways(fills), f_send, f_recv)
    ring_a.start()

    def to_part(src, dst, k, peer):
        return pltpu.make_async_remote_copy(
            src_ref=src, dst_ref=dst, send_sem=m_send.at[k], recv_sem=m_recv.at[k],
            device_id={"tm": peer}, device_id_type=MESH,
        )

    def diag_part(out, sep_factor, terms):
        out[...] = jnp.zeros_like(out)

        @pl.loop(0, rows // chunk)
        def _(i):
            at = pl.multiple_of(i * chunk, chunk)
            total = jnp.zeros((chunk, 1), jnp.float32)
            for left, right in terms:
                total += jnp.sum(
                    left(at).astype(jnp.float32) * right(at).astype(jnp.float32),
                    axis=1, keepdims=True,
                )
            spot = lax.broadcasted_iota(jnp.int32, (chunk, width), 1) == (
                lax.broadcasted_iota(jnp.int32, (chunk, width), 0) + (z * rows + at)
            )
            values = sep[pl.ds(at, chunk), :] * sep_factor - total
            out[...] += jnp.sum(jnp.where(spot, values, 0.0), axis=0, keepdims=True)

    def spread(edge, edge_in, diags, peer, k, sems):
        copy = pltpu.make_async_remote_copy(
            src_ref=edge, dst_ref=edge_in, send_sem=e_send.at[k], recv_sem=e_recv.at[k],
            device_id={"tm": peer}, device_id_type=MESH,
        )
        copy.start()
        copy.wait()
        diags[z] = edge[...] + edge_in[...]
        for s in range(1, ring):
            spread_copy(diags, s, sems).start()

    def spread_copy(diags, s, sems):
        return pltpu.make_async_remote_copy(
            src_ref=diags.at[z], dst_ref=diags.at[z], send_sem=sems[0].at[s - 1],
            recv_sem=sems[1].at[s - 1],
            device_id={"space": lax.rem(z + s, ring)}, device_id_type=MESH,
        )

    def pivot_scale(diags, sems):
        for s in range(1, ring):
            spread_copy(diags, s, sems).wait_recv()
        values = diags[0]
        for s in range(1, ring):
            values += diags[s]
        return (1.0 / jnp.maximum(values, 1.0)).astype(jnp.bfloat16).astype(jnp.float32)

    def scale_rows(source, factors, out):
        @pl.loop(0, rows // chunk)
        def _(i):
            at = pl.multiple_of(i * chunk, chunk)
            out(at)[...] = (source(at)[...].astype(jnp.float32) * factors).astype(jnp.bfloat16)

    def product(left, right, take):
        @pl.loop(0, width // tile)
        def _(j):
            at = pl.multiple_of(j * tile, tile)
            take(
                pl.ds(at, tile),
                lax.dot_general(
                    left[...], right[pl.ds(at, tile), :], (((1,), (1,)), ((), ())),
                    preferred_element_type=jnp.float32,
                ),
            )

    reciprocal = 1.0 / diag_ref[...]
    for which in (OWN, PREV):
        scale_rows(
            lambda at: pair.at[which, pl.ds(pl.multiple_of(z * rows + at, chunk), chunk)],
            reciprocal,
            lambda at: scaled.at[which, pl.ds(at, chunk)],
        )

    def form_rows(which):
        return (
            lambda at: scaled[which, pl.ds(at, chunk), :],
            lambda at: pair[which, pl.ds(pl.multiple_of(z * rows + at, chunk), chunk), :],
        )

    first, second = 1 - odd, odd
    diag_part(edge, (1 - odd).astype(jnp.float32), [form_rows(second)])
    spread(edge, edge_in, diags, sib, 0, (d_send, d_recv))
    ring_a.run()

    sign = jnp.where(t == 0, 0.0, -1.0)
    my_links = links.at[mine(z)]
    my_fills = fills.at[mine(z)]

    def take_link(at, value):
        my_links[:, at] = (value * sign).astype(jnp.bfloat16)

    product(scaled.at[first], pair.at[second], take_link)
    ring_w.start()
    scale1 = pivot_scale(diags, (d_send, d_recv))
    scale_rows(
        lambda at: my_links.at[pl.ds(at, chunk)], scale1, lambda at: links_scaled.at[pl.ds(at, chunk)]
    )
    hand = to_part(links_scaled, sibling, 0, sib)

    @pl.when(jnp.logical_not(inner))
    def _():
        hand.start()

    @pl.when(inner)
    def _():
        diag_part(
            edge2, odd.astype(jnp.float32),
            [
                form_rows(first),
                (
                    lambda at: links_scaled[pl.ds(at, chunk), :],
                    lambda at: links[pl.ds(pl.multiple_of(z * rows + at, chunk), chunk), :],
                ),
            ],
        )
        spread(edge2, edge2_in, diags2, across, 1, (d2_send, d2_recv))

    def take_own(at, value):
        schur_ref[:, at] = sep[:, at] - value

    def take_prev(at, value):
        update[:, at] = value.astype(jnp.bfloat16)

    def take_prev_wide(at, value):
        sep[:, at] = value

    product(scaled.at[OWN], pair.at[OWN], take_own)
    send_update = to_part(update, update_in, 1, before)

    @pl.when(is_odd)
    def _():
        product(scaled.at[PREV], pair.at[PREV], take_prev)
        send_update.start()

    @pl.when(jnp.logical_not(is_odd))
    def _():
        product(scaled.at[PREV], pair.at[PREV], take_prev_wide)
        link_ref[...] = my_links[...]

    ring_w.run()
    hand_fill = to_part(fills_scaled, handed, 2, after)

    @pl.when(inner)
    def _():
        hand.wait_recv()

        def take_fill(at, value):
            my_fills[:, at] = (-value).astype(jnp.bfloat16)

        product(sibling, links, take_fill)
        ring_f.start()
        scale2 = pivot_scale(diags2, (d2_send, d2_recv))
        scale_rows(
            lambda at: my_fills.at[pl.ds(at, chunk)], scale2,
            lambda at: fills_scaled.at[pl.ds(at, chunk)],
        )

    @pl.when(role == 1)
    def _():
        hand_fill.start()
        link_ref[...] = my_fills[...]

    @pl.when(is_odd)
    def _():
        def take(at, value):
            schur_ref[:, at] -= value

        product(links_scaled, links, take)

    @pl.when(jnp.logical_not(is_odd))
    def _():
        def take(at, value):
            update[:, at] = (sep[:, at] + value).astype(jnp.bfloat16)

        product(links_scaled, links, take)
        send_update.start()

    @pl.when(inner)
    def _():
        ring_f.run()

    send_far = to_part(far, far_in, 3, before2)
    send_last = to_part(last, last_in, 4, after)
    send_final = to_part(final, final_in, 5, after)

    @pl.when(role == 1)
    def _():
        def take(at, value):
            far[:, at] = value.astype(jnp.bfloat16)

        product(fills_scaled, fills, take)
        send_far.start()

    @pl.when(role == 2)
    def _():
        def take(at, value):
            last[:, at] = value.astype(jnp.bfloat16)

        product(fills_scaled, fills, take)
        send_last.start()
        hand_fill.wait_recv()

        def take_final(at, value):
            final[:, at] = (-value).astype(jnp.bfloat16)

        product(handed, fills, take_final)
        send_final.start()

    send_update.wait_recv()

    @pl.when(t != parts - 1)
    def _():
        schur_ref[...] -= update_in[...].astype(jnp.float32)

    @pl.when(role == 3)
    def _():
        send_far.wait_recv()
        send_last.wait_recv()

        @pl.when(t != parts - 1)
        def _():
            schur_ref[...] -= far_in[...].astype(jnp.float32)

        schur_ref[...] -= last_in[...].astype(jnp.float32)
        send_final.wait_recv()
        link_ref[...] = final_in[...]

    ring_a.drain()
    ring_w.drain()
    send_update.wait_send()
    for s in range(1, ring):
        spread_copy(diags, s, (d_send, d_recv)).wait_send()

    @pl.when(inner)
    def _():
        ring_f.drain()
        for s in range(1, ring):
            spread_copy(diags2, s, (d2_send, d2_recv)).wait_send()

    @pl.when(jnp.logical_not(inner))
    def _():
        hand.wait_send()

    @pl.when(role == 1)
    def _():
        hand_fill.wait_send()
        send_far.wait_send()

    @pl.when(role == 2)
    def _():
        send_last.wait_send()
        send_final.wait_send()


def solution(mesh):
    ring, parts = mesh.shape["space"], mesh.shape["tm"]

    def on_device(sep_block, own_couple, prev_couple, inner_diag):
        rows, width = sep_block.shape[1:]

        def block(kind, *lead):
            return pltpu.VMEM((*lead, rows, width), kind)

        def full(*lead):
            return pltpu.VMEM((*lead, width, width), jnp.bfloat16)

        line = pltpu.VMEM((1, width), jnp.float32)
        lines = pltpu.VMEM((ring, 1, width), jnp.float32)
        half = jnp.bfloat16
        hops = pltpu.SemaphoreType.DMA((4 * (ring // 2),))
        peers = pltpu.SemaphoreType.DMA((ring - 1,))
        schur, link = pl.pallas_call(
            functools.partial(kernel, ring, parts),
            out_shape=(
                jax.ShapeDtypeStruct((rows, width), jnp.float32),
                jax.ShapeDtypeStruct((rows, width), half),
            ),
            in_specs=[pl.BlockSpec(memory_space=pl.ANY)] * 3
            + [pl.BlockSpec(memory_space=pltpu.VMEM)],
            out_specs=(pl.BlockSpec(memory_space=pltpu.VMEM),) * 2,
            scratch_shapes=[
                block(jnp.float32), full(2), block(half, 2), full(), block(half), full(), block(half),
                block(half), block(half), block(half), block(half), block(half), block(half),
                block(half), block(half), block(half), block(half),
                line, line, lines, line, line, lines,
                pltpu.SemaphoreType.DMA((3,)), hops, hops, hops, hops, hops, hops,
                peers, peers, peers, peers,
                pltpu.SemaphoreType.DMA((2,)), pltpu.SemaphoreType.DMA((2,)),
                pltpu.SemaphoreType.DMA((6,)), pltpu.SemaphoreType.DMA((6,)),
            ],
            compiler_params=pltpu.CompilerParams(
                collective_id=0, has_side_effects=True, vmem_limit_bytes=56 * 2**20
            ),
            cost_estimate=pl.CostEstimate(
                flops=7 * 2 * rows * width * width, bytes_accessed=10 * rows * width, transcendentals=0
            ),
        )(sep_block[0], own_couple[0], prev_couple[0], inner_diag)
        return schur[None], link[None]

    placed = (P("tm", "space", None), P("tm", "space", None), P("tm", "space", None), P("tm", None))
    return jax.shard_map(
        on_device,
        mesh=mesh,
        in_specs=placed,
        out_specs=(P("tm", "space", None), P("tm", "space", None)),
        check_vma=False,
    )
```

```python
import functools

import jax
import jax.numpy as jnp
from jax import lax
from jax.experimental import pallas as pl
from jax.experimental.pallas import tpu as pltpu
from jax.sharding import PartitionSpec as P

MESH = pl.DeviceIdType.MESH
OWN, PREV = 0, 1


def kernel(
    ring, parts, sep_hbm, own_hbm, prev_hbm, diag_ref, schur_ref, link_ref,
    sep, pair, scaled, links, links_scaled, sibling, fills, fills_scaled, handed,
    link_cells, form_cells, fill_cells, square_cells, update, update_in,
    far, far_in, last, last_in, final, final_in,
    link_out, form_out, fill_out, square_out,
    edge, edge_in, diags, edge2, edge2_in, diags2,
    load_sem, a_send, a_recv, w_send, w_recv, f_send, f_recv,
    d_send, d_recv, d2_send, d2_recv, e_send, e_recv, hand_send, hand_recv,
    r_send, r_recv, m_send, m_recv, t_send, t_recv,
):
    rows, width = sep.shape
    chunk = 16
    z = lax.axis_index("space")
    t = lax.axis_index("tm")
    odd = lax.rem(t, 2)
    role = lax.rem(t, 4)
    is_odd = odd == 1
    inner = jnp.logical_or(role == 1, role == 2)
    sib = t + 1 - 2 * odd
    across = lax.rem(t + 2 * odd - 1 + parts, parts)
    before = lax.rem(t + parts - 1, parts)
    before2 = lax.rem(t + parts - 2, parts)
    after = lax.rem(t + 1, parts)
    after2 = lax.rem(t + 2, parts)
    first, second = 1 - odd, odd

    barrier = pltpu.get_barrier_semaphore()
    for k in range(1, ring):
        pl.semaphore_signal(
            barrier, inc=1, device_id={"space": lax.rem(z + k, ring)}, device_id_type=MESH
        )
    for peer in (before, before2, after, after2):
        pl.semaphore_signal(barrier, inc=1, device_id={"tm": peer}, device_id_type=MESH)

    def near(d):
        return lax.rem(z + d + ring, ring)

    def row_slice(d):
        return pl.ds(pl.multiple_of(near(d) * rows, rows), rows)

    def cell_columns(j):
        return slice(j * rows, (j + 1) * rows)

    loads = [
        pltpu.make_async_copy(own_hbm, pair.at[OWN, row_slice(0)], load_sem.at[0]),
        pltpu.make_async_copy(prev_hbm, pair.at[PREV, row_slice(0)], load_sem.at[1]),
        pltpu.make_async_copy(sep_hbm, sep, load_sem.at[2]),
    ]
    for load in loads:
        load.start()
    for load in loads:
        load.wait()
    pl.semaphore_wait(barrier, ring + 3)

    def along(src, dst, way, send_sem, recv_sem):
        return pltpu.make_async_remote_copy(
            src_ref=src, dst_ref=dst, send_sem=send_sem, recv_sem=recv_sem,
            device_id={"space": near(way)}, device_id_type=MESH,
        )

    class Ring:
        def __init__(self, streams, send_sem, recv_sem):
            self.streams = streams
            self.sems = send_sem, recv_sem

        def at(self, s, step):
            buf, offset, count, way, _ = self.streams[s]
            at = s * (ring // 2) + step - 1
            slot = near(-way * (step - 1))
            piece = buf.at[pl.ds(pl.multiple_of(slot * rows + offset, chunk), count)]
            return along(piece, piece, way, self.sems[0].at[at], self.sems[1].at[at])

        def start(self):
            for s in range(len(self.streams)):
                self.at(s, 1).start()

        def arrive(self, step, which=None):
            for s, stream in enumerate(self.streams):
                if step <= stream[4] and (which is None or s in which):
                    self.at(s, step).wait_recv()
                    if step < stream[4]:
                        self.at(s, step + 1).start()

        def drain(self):
            for s, stream in enumerate(self.streams):
                for step in range(1, stream[4] + 1):
                    self.at(s, step).wait_send()

    half = rows // 2
    ring_a = Ring(
        [
            (pair.at[first], 0, rows, 1, 2),
            (pair.at[first], 0, rows, -1, 2),
            (pair.at[second], 0, rows, 1, 2),
            (pair.at[second], 0, rows, -1, 2),
        ],
        a_send, a_recv,
    )
    ring_w = Ring(
        [
            (links, 0, half, 1, 2),
            (links, 0, half, -1, 2),
            (links, half, half, 1, 2),
            (links, half, half, -1, 2),
        ],
        w_send, w_recv,
    )
    ring_f = Ring(
        [
            (fills, 0, half, 1, ring // 2),
            (fills, half, half, -1, ring // 2),
            (fills, 0, half, -1, ring // 2 - 1),
            (fills, half, half, 1, ring // 2 - 1),
        ],
        f_send, f_recv,
    )
    ring_a.start()

    def to_part(src, dst, peer, send_sem, recv_sem):
        return pltpu.make_async_remote_copy(
            src_ref=src, dst_ref=dst, send_sem=send_sem, recv_sem=recv_sem,
            device_id={"tm": peer}, device_id_type=MESH,
        )

    def diag_part(out, sep_factor, terms):
        out[...] = jnp.zeros_like(out)

        @pl.loop(0, rows // chunk)
        def _(i):
            at = pl.multiple_of(i * chunk, chunk)
            total = jnp.zeros((chunk, 1), jnp.float32)
            for left, right in terms:
                total += jnp.sum(
                    left(at).astype(jnp.float32) * right(at).astype(jnp.float32),
                    axis=1, keepdims=True,
                )
            spot = lax.broadcasted_iota(jnp.int32, (chunk, width), 1) == (
                lax.broadcasted_iota(jnp.int32, (chunk, width), 0) + (z * rows + at)
            )
            values = sep[pl.ds(at, chunk), :] * sep_factor - total
            out[...] += jnp.sum(jnp.where(spot, values, 0.0), axis=0, keepdims=True)

    def spread(edge, edge_in, diags, peer, k, sems):
        copy = to_part(edge, edge_in, peer, e_send.at[k], e_recv.at[k])
        copy.start()
        copy.wait()
        diags[z] = edge[...] + edge_in[...]
        for s in range(1, ring):
            spread_copy(diags, s, sems).start()

    def spread_copy(diags, s, sems):
        return along(diags.at[z], diags.at[z], s, sems[0].at[s - 1], sems[1].at[s - 1])

    def pivot_scale(diags, sems):
        for s in range(1, ring):
            spread_copy(diags, s, sems).wait_recv()
        values = diags[0]
        for s in range(1, ring):
            values += diags[s]
        return (1.0 / jnp.maximum(values, 1.0)).astype(jnp.bfloat16).astype(jnp.float32)

    def scale_rows(source, factors, out):
        @pl.loop(0, rows // chunk)
        def _(i):
            at = pl.ds(pl.multiple_of(i * chunk, chunk), chunk)
            out[at, :] = (source[at, :].astype(jnp.float32) * factors).astype(jnp.bfloat16)

    def dot(left, right):
        return lax.dot_general(
            left[...], right[...], (((1,), (1,)), ((), ())), preferred_element_type=jnp.float32
        )

    lanes = {0: slice(0, rows), 1: slice(rows, 2 * rows)}
    scaled_at = {0: 0, -1: 1, 1: 2, 2: 3}

    def put(cells, index, value, part=0):
        cells[index, :, lanes[part]] = value.astype(jnp.bfloat16)

    def returned(out, cells, k, group, long_way):
        way = (-1, 1, long_way)[k]
        col = (2, -2, -long_way)[k]
        at = 3 * group + k
        return along(out.at[k], cells.at[near(col)], way, r_send.at[at], r_recv.at[at])

    reciprocal = 1.0 / diag_ref[...]

    def scale_pair(which, d):
        scale_rows(pair.at[which, row_slice(d)], reciprocal, scaled.at[which, scaled_at[d]])

    def pair_rows(which, d):
        return pair.at[which, row_slice(d)]

    def link_rows(d):
        return links.at[row_slice(d)]

    scale_pair(OWN, 0)
    scale_pair(PREV, 0)

    def form_rows(which):
        mine = pair.at[which, row_slice(0)]
        return (
            lambda at: scaled[which, 0, pl.ds(at, chunk), :],
            lambda at: mine[pl.ds(at, chunk), :],
        )

    diag_part(edge, (1 - odd).astype(jnp.float32), [form_rows(second)])
    spread(edge, edge_in, diags, sib, 0, (d_send, d_recv))

    sign = jnp.where(t == 0, 0.0, -1.0)

    def link_cell(d):
        put(link_cells, near(d), dot(scaled.at[first, 0], pair_rows(second, d)) * sign)

    def form_cell(d):
        for which in (OWN, PREV):
            put(form_cells, near(d), dot(scaled.at[which, 0], pair_rows(which, d)), which)

    link_cell(0)
    form_cell(0)
    ring_a.arrive(1)
    for d in (-1, 1):
        scale_pair(OWN, d)
        scale_pair(PREV, d)
        link_cell(d)
        form_cell(d)
    ring_a.arrive(2, (0, 1))
    scale_pair(first, 2)
    ring_a.arrive(2, (2, 3))
    for k, (row, col) in enumerate(((-1, 2), (1, -2), (2, -2))):
        put(link_out, k, dot(scaled.at[first, scaled_at[row]], pair_rows(second, col)) * sign)
        returned(link_out, link_cells, k, 0, 2).start()
    link_cell(-2)
    link_cell(2)
    scale_pair(second, 2)
    for k, (row, col) in enumerate(((-1, 2), (1, -2))):
        for which in (OWN, PREV):
            put(form_out, k, dot(scaled.at[which, scaled_at[row]], pair_rows(which, col)), which)
        returned(form_out, form_cells, k, 1, -2).start()
    for which in (OWN, PREV):
        put(form_out, 2, dot(pair_rows(which, -2), scaled.at[which, scaled_at[2]]), which)
    returned(form_out, form_cells, 2, 1, -2).start()

    my_links = link_rows(0)
    my_fills = fills.at[row_slice(0)]
    for k in range(3):
        returned(link_out, link_cells, k, 0, 2).wait_recv()
    for j in range(ring):
        my_links[:, cell_columns(j)] = link_cells[j, :, lanes[0]]
    ring_w.start()

    scale1 = pivot_scale(diags, (d_send, d_recv))

    def hand(d):
        k = scaled_at[d]
        return to_part(links_scaled.at[k], sibling.at[k], sib, hand_send.at[k], hand_recv.at[k])

    def scale_link(d):
        scale_rows(link_rows(d), scale1, links_scaled.at[scaled_at[d]])

        @pl.when(jnp.logical_not(inner))
        def _():
            hand(d).start()

    def square_cell(d):
        put(square_cells, near(d), dot(links_scaled.at[0], link_rows(d)))

    def fill_cell(d):
        put(fill_cells, near(d), -dot(sibling.at[0], link_rows(d)))

    scale_link(0)

    @pl.when(inner)
    def _():
        mine = link_rows(0)
        diag_part(
            edge2, odd.astype(jnp.float32),
            [
                form_rows(first),
                (
                    lambda at: links_scaled[0, pl.ds(at, chunk), :],
                    lambda at: mine[pl.ds(at, chunk), :],
                ),
            ],
        )
        spread(edge2, edge2_in, diags2, across, 1, (d2_send, d2_recv))
        hand(0).wait_recv()
        fill_cell(0)

    square_cell(0)
    ring_w.arrive(1)
    for d in (-1, 1):
        scale_link(d)

    @pl.when(inner)
    def _():
        fill_cell(-1)
        fill_cell(1)

    for d in (-1, 1):
        square_cell(d)
    form_cell(-2)
    form_cell(2)

    @pl.when(jnp.logical_not(is_odd))
    def _():
        link_ref[...] = my_links[...]

    ring_w.arrive(2)
    scale_link(2)

    @pl.when(inner)
    def _():
        for d in (-1, 1, 2):
            hand(d).wait_recv()
        for k, (row, col) in enumerate(((-1, 2), (1, -2), (2, -2))):
            put(fill_out, k, -dot(sibling.at[scaled_at[row]], link_rows(col)))
            returned(fill_out, fill_cells, k, 2, 2).start()
        fill_cell(-2)
        fill_cell(2)

    for k, (row, col) in enumerate(((-1, 2), (1, -2))):
        put(square_out, k, dot(links_scaled.at[scaled_at[row]], link_rows(col)))
        returned(square_out, square_cells, k, 3, -2).start()
    put(square_out, 2, dot(link_rows(-2), links_scaled.at[scaled_at[2]]))
    returned(square_out, square_cells, 2, 3, -2).start()

    hand_fill = to_part(fills_scaled, handed, after, m_send.at[0], m_recv.at[0])

    @pl.when(inner)
    def _():
        for k in range(3):
            returned(fill_out, fill_cells, k, 2, 2).wait_recv()
        for j in range(ring):
            my_fills[:, cell_columns(j)] = fill_cells[j, :, lanes[0]]
        ring_f.start()
        scale_rows(my_fills, pivot_scale(diags2, (d2_send, d2_recv)), fills_scaled)

    @pl.when(role == 1)
    def _():
        hand_fill.start()
        link_ref[...] = my_fills[...]

    square_cell(-2)
    square_cell(2)
    for k in range(3):
        returned(form_out, form_cells, k, 1, -2).wait_recv()
        returned(square_out, square_cells, k, 3, -2).wait_recv()
    send_update = to_part(update, update_in, before, m_send.at[1], m_recv.at[1])

    @pl.when(is_odd)
    def _():
        for j in range(ring):
            at = cell_columns(j)
            taken = form_cells[j, :, lanes[OWN]].astype(jnp.float32)
            taken += square_cells[j, :, lanes[0]].astype(jnp.float32)
            schur_ref[:, at] = sep[:, at] - taken
            update[j, :, lanes[0]] = form_cells[j, :, lanes[PREV]]

    @pl.when(jnp.logical_not(is_odd))
    def _():
        for j in range(ring):
            at = cell_columns(j)
            schur_ref[:, at] = sep[:, at] - form_cells[j, :, lanes[OWN]].astype(jnp.float32)
            total = form_cells[j, :, lanes[PREV]].astype(jnp.float32)
            total += square_cells[j, :, lanes[0]].astype(jnp.float32)
            put(update, j, total)

    send_update.start()

    order = [0]
    for step in range(1, ring // 2):
        order += [-step, step]
    order.append(ring // 2)

    def handed_on(src, dst, peer, group, i):
        j = near(order[i])
        at = group * ring + i
        return to_part(src.at[j], dst.at[j], peer, t_send.at[at], t_recv.at[at])

    def last_cells(which):
        @pl.when(role == 1)
        def _():
            for i in which:
                put(far, near(order[i]), dot(fills_scaled, fills.at[row_slice(order[i])]))
                handed_on(far, far_in, before2, 0, i).start()

        @pl.when(role == 2)
        def _():
            for i in which:
                right = fills.at[row_slice(order[i])]
                put(last, near(order[i]), dot(fills_scaled, right))
                handed_on(last, last_in, after, 1, i).start()
                put(final, near(order[i]), -dot(handed, right))
                handed_on(final, final_in, after, 2, i).start()

    def take_update():
        send_update.wait_recv()

        @pl.when(t != parts - 1)
        def _():
            for j in range(ring):
                schur_ref[:, cell_columns(j)] -= update_in[j, :, lanes[0]].astype(jnp.float32)

    @pl.when(role == 2)
    def _():
        hand_fill.wait_recv()

    last_cells([0])

    @pl.when(inner)
    def _():
        ring_f.arrive(1)

    last_cells([1, 2])

    @pl.when(inner)
    def _():
        ring_f.arrive(2)

    take_update()
    last_cells([3, 4])

    @pl.when(inner)
    def _():
        ring_f.arrive(3)

    last_cells([5, 6])

    @pl.when(inner)
    def _():
        ring_f.arrive(4)

    last_cells([7])

    @pl.when(role == 3)
    def _():
        for i in range(ring):
            handed_on(far, far_in, before2, 0, i).wait_recv()
            handed_on(last, last_in, after, 1, i).wait_recv()
            handed_on(final, final_in, after, 2, i).wait_recv()
        for j in range(ring):
            at = cell_columns(j)
            schur_ref[:, at] -= last_in[j, :, lanes[0]].astype(jnp.float32)
            link_ref[:, at] = final_in[j, :, lanes[0]]

        @pl.when(t != parts - 1)
        def _():
            for j in range(ring):
                schur_ref[:, cell_columns(j)] -= far_in[j, :, lanes[0]].astype(jnp.float32)

    ring_a.drain()
    ring_w.drain()
    send_update.wait_send()
    for s in range(1, ring):
        spread_copy(diags, s, (d_send, d_recv)).wait_send()
    for k in range(3):
        returned(link_out, link_cells, k, 0, 2).wait_send()
        returned(form_out, form_cells, k, 1, -2).wait_send()
        returned(square_out, square_cells, k, 3, -2).wait_send()

    @pl.when(inner)
    def _():
        ring_f.drain()
        for k in range(3):
            returned(fill_out, fill_cells, k, 2, 2).wait_send()
        for s in range(1, ring):
            spread_copy(diags2, s, (d2_send, d2_recv)).wait_send()

    @pl.when(jnp.logical_not(inner))
    def _():
        for d in scaled_at:
            hand(d).wait_send()

    @pl.when(role == 1)
    def _():
        hand_fill.wait_send()
        for i in range(ring):
            handed_on(far, far_in, before2, 0, i).wait_send()

    @pl.when(role == 2)
    def _():
        for i in range(ring):
            handed_on(last, last_in, after, 1, i).wait_send()
            handed_on(final, final_in, after, 2, i).wait_send()


def solution(mesh):
    ring, parts = mesh.shape["space"], mesh.shape["tm"]

    def on_device(sep_block, own_couple, prev_couple, inner_diag):
        rows, width = sep_block.shape[1:]

        def block(kind, *lead):
            return pltpu.VMEM((*lead, rows, width), kind)

        def full(*lead):
            return pltpu.VMEM((*lead, width, width), jnp.bfloat16)

        line = pltpu.VMEM((1, width), jnp.float32)
        lines = pltpu.VMEM((ring, 1, width), jnp.float32)
        half = jnp.bfloat16
        dma = lambda count: pltpu.SemaphoreType.DMA((count,))
        hops = dma(4 * (ring // 2))

        def cells(count, parts_of):
            lanes = -(-parts_of * rows // 128) * 128
            return pltpu.VMEM((count, rows, lanes), half)

        schur, link = pl.pallas_call(
            functools.partial(kernel, ring, parts),
            out_shape=(
                jax.ShapeDtypeStruct((rows, width), jnp.float32),
                jax.ShapeDtypeStruct((rows, width), half),
            ),
            in_specs=[pl.BlockSpec(memory_space=pl.ANY)] * 3
            + [pl.BlockSpec(memory_space=pltpu.VMEM)],
            out_specs=(pl.BlockSpec(memory_space=pltpu.VMEM),) * 2,
            scratch_shapes=[
                block(jnp.float32), full(2), block(half, 2, 4), full(), block(half, 4), block(half, 4),
                full(), block(half), block(half),
                cells(ring, 1), cells(ring, 2), cells(ring, 1), cells(ring, 1),
                *[cells(ring, 1)] * 8,
                cells(3, 1), cells(3, 2), cells(3, 1), cells(3, 1),
                line, line, lines, line, line, lines,
                dma(3), hops, hops, hops, hops, hops, hops,
                dma(ring - 1), dma(ring - 1), dma(ring - 1), dma(ring - 1),
                dma(2), dma(2), dma(4), dma(4), dma(12), dma(12), dma(2), dma(2),
                dma(3 * ring), dma(3 * ring),
            ],
            compiler_params=pltpu.CompilerParams(
                collective_id=0, has_side_effects=True, vmem_limit_bytes=56 * 2**20
            ),
            cost_estimate=pl.CostEstimate(
                flops=7 * 2 * rows * width * width, bytes_accessed=10 * rows * width, transcendentals=0
            ),
        )(sep_block[0], own_couple[0], prev_couple[0], inner_diag)
        return schur[None], link[None]

    placed = (P("tm", "space", None), P("tm", "space", None), P("tm", "space", None), P("tm", None))
    return jax.shard_map(
        on_device,
        mesh=mesh,
        in_specs=placed,
        out_specs=(P("tm", "space", None), P("tm", "space", None)),
        check_vma=False,
    )
```

```python
import functools

import jax
import jax.numpy as jnp
from jax import lax
from jax.experimental import pallas as pl
from jax.experimental.pallas import tpu as pltpu
from jax.sharding import PartitionSpec as P

MESH = pl.DeviceIdType.MESH
OWN, PREV = 0, 1


def kernel(
    ring, parts, sep_hbm, own_hbm, prev_hbm, diag_ref, schur_ref, link_ref,
    sep, pair, scaled, link, link_scaled, sibling, turned, fill_scaled, handed,
    passed, passed_in, last, last_in, left, left_wide, far_left,
    link_cells, form_cells, fill_cells, square_cells, final_cells, update_in,
    reciprocal, edge, edge_in, diags, edge2, edge2_in, diags2,
    load_sem, y_send, y_recv, x_send, x_recv,
    d_send, d_recv, d2_send, d2_recv, e_send, e_recv, m_send, m_recv, t_send, t_recv, go,
):
    rows, width = sep.shape
    chunk = 16
    tile = 512
    z = lax.axis_index("space")
    t = lax.axis_index("tm")
    odd = lax.rem(t, 2)
    role = lax.rem(t, 4)
    is_odd = odd == 1
    inner = jnp.logical_or(role == 1, role == 2)
    outer = jnp.logical_not(inner)
    sib = t + 1 - 2 * odd
    across = lax.rem(t + 2 * odd - 1 + parts, parts)
    before = lax.rem(t + parts - 1, parts)
    after = lax.rem(t + 1, parts)
    first, second = 1 - odd, odd

    barrier = pltpu.get_barrier_semaphore()
    for k in range(1, ring):
        pl.semaphore_signal(
            barrier, inc=1, device_id={"space": lax.rem(z + k, ring)}, device_id_type=MESH
        )
    for peer in (before, after):
        pl.semaphore_signal(barrier, inc=1, device_id={"tm": peer}, device_id_type=MESH)

    def near(d):
        return lax.rem(z + d + ring, ring)

    def row_slice(d):
        return pl.ds(pl.multiple_of(near(d) * rows, rows), rows)

    def cell_columns(j):
        return slice(j * rows, (j + 1) * rows)

    loads = [
        pltpu.make_async_copy(own_hbm, pair.at[OWN, row_slice(0)], load_sem.at[0]),
        pltpu.make_async_copy(prev_hbm, pair.at[PREV, row_slice(0)], load_sem.at[1]),
        pltpu.make_async_copy(sep_hbm, sep, load_sem.at[2]),
    ]
    for load in loads:
        load.start()
    for load in loads:
        load.wait()
    pl.semaphore_wait(barrier, ring + 1)

    def along(src, dst, way, send_sem, recv_sem):
        return pltpu.make_async_remote_copy(
            src_ref=src, dst_ref=dst, send_sem=send_sem, recv_sem=recv_sem,
            device_id={"space": near(way)}, device_id_type=MESH,
        )

    def to_part(src, dst, peer, send_sem, recv_sem):
        return pltpu.make_async_remote_copy(
            src_ref=src, dst_ref=dst, send_sem=send_sem, recv_sem=recv_sem,
            device_id={"tm": peer}, device_id_type=MESH,
        )

    class Ring:
        def __init__(self, buf, pieces, send_sem, recv_sem):
            size = rows // pieces
            self.streams = []
            for i in range(pieces):
                long_way = 1 if i % 2 == 0 else -1
                self.streams.append((buf, i * size, size, long_way, ring // 2))
                self.streams.append((buf, i * size, size, -long_way, ring // 2 - 1))
            self.sems = send_sem, recv_sem

        def at(self, s, step):
            buf, offset, count, way, _ = self.streams[s]
            at = s * (ring // 2) + step - 1
            slot = near(-way * (step - 1))
            piece = buf.at[pl.ds(pl.multiple_of(slot * rows + offset, chunk), count)]
            return along(piece, piece, way, self.sems[0].at[at], self.sems[1].at[at])

        def start(self, begin=0, end=None):
            for s in range(len(self.streams))[begin:end]:
                self.at(s, 1).start()

        def arrive(self, step):
            for s, stream in enumerate(self.streams):
                if step <= stream[4]:
                    self.at(s, step).wait_recv()
                    if step < stream[4]:
                        self.at(s, step + 1).start()

        def drain(self):
            for s, stream in enumerate(self.streams):
                for step in range(1, stream[4] + 1):
                    self.at(s, step).wait_send()

    x_all = pair.at[first]
    y_all = pair.at[second]
    ring_y = Ring(y_all, 2, y_send, y_recv)
    ring_x = Ring(x_all, 4, x_send, x_recv)
    ring_y.start()

    def diag_part(out, sep_factor, terms):
        out[...] = jnp.zeros_like(out)

        @pl.loop(0, rows // chunk)
        def _(i):
            at = pl.multiple_of(i * chunk, chunk)
            total = jnp.zeros((chunk, 1), jnp.float32)
            for left_rows, right_rows in terms:
                total += jnp.sum(
                    left_rows[pl.ds(at, chunk), :].astype(jnp.float32)
                    * right_rows[pl.ds(at, chunk), :].astype(jnp.float32),
                    axis=1, keepdims=True,
                )
            spot = lax.broadcasted_iota(jnp.int32, (chunk, width), 1) == (
                lax.broadcasted_iota(jnp.int32, (chunk, width), 0) + (z * rows + at)
            )
            values = sep[pl.ds(at, chunk), :] * sep_factor - total
            out[...] += jnp.sum(jnp.where(spot, values, 0.0), axis=0, keepdims=True)

    def edge_copy(edge, edge_in, peer, k):
        return to_part(edge, edge_in, peer, e_send.at[k], e_recv.at[k])

    def spread_copy(diags, s, sems):
        return along(diags.at[z], diags.at[z], s, sems[0].at[s - 1], sems[1].at[s - 1])

    def spread(edge, edge_in, diags, peer, k, sems):
        edge_copy(edge, edge_in, peer, k).wait()
        diags[z] = edge[...] + edge_in[...]
        for s in range(1, ring):
            spread_copy(diags, s, sems).start()

    def pivot_scale(diags, sems):
        for s in range(1, ring):
            spread_copy(diags, s, sems).wait_recv()
        values = diags[0]
        for s in range(1, ring):
            values += diags[s]
        return (1.0 / jnp.maximum(values, 1.0)).astype(jnp.bfloat16).astype(jnp.float32)

    def scale_rows(source, factors, out):
        @pl.loop(0, rows // chunk)
        def _(i):
            at = pl.ds(pl.multiple_of(i * chunk, chunk), chunk)
            out[at, :] = (source[at, :].astype(jnp.float32) * factors).astype(jnp.bfloat16)

    def dot(left_rows, right_rows):
        return lax.dot_general(
            left_rows[...], right_rows[...], (((1,), (1,)), ((), ())),
            preferred_element_type=jnp.float32,
        )

    def times(left_rows, matrix, take):
        @pl.loop(0, width // tile)
        def _(j):
            at = pl.ds(pl.multiple_of(j * tile, tile), tile)
            take(at, jnp.dot(left_rows[...], matrix[:, at], preferred_element_type=jnp.float32))

    def times_turned(left_rows, matrix, take):
        @pl.loop(0, width // tile)
        def _(j):
            at = pl.ds(pl.multiple_of(j * tile, tile), tile)
            take(at, dot(left_rows, matrix.at[at]))

    def scaled_into(out, factors):
        def take(at, value):
            out[:, at] = (value * factors[:, at]).astype(jnp.bfloat16)

        return take

    cell = slice(0, rows)

    def put(cells, d, value):
        cells[near(d), :, cell] = value.astype(jnp.bfloat16)

    def x_rows(d):
        return x_all.at[row_slice(d)]

    def y_rows(d):
        return y_all.at[row_slice(d)]

    reach = {0: (0,), 4: (ring // 2,)}
    for step in range(1, ring // 2):
        reach[step] = (-step, step)

    reciprocal[...] = 1.0 / diag_ref[...]
    x_scaled, y_scaled = scaled.at[0], scaled.at[1]
    scale_rows(y_rows(0), reciprocal[...], y_scaled)
    scale_rows(x_rows(0), reciprocal[...], x_scaled)
    diag_part(edge, (1 - odd).astype(jnp.float32), [(y_scaled, y_rows(0))])
    edge_copy(edge, edge_in, sib, 0).start()
    spread(edge, edge_in, diags, sib, 0, (d_send, d_recv))

    sign = jnp.where(t == 0, 0.0, -1.0)

    def link_and_form(step):
        for d in reach[step]:
            put(link_cells, d, dot(x_scaled, y_rows(d)) * sign)
            put(form_cells, d, dot(y_scaled, y_rows(d)))

    link_and_form(0)
    for step in (1, 2, 3):
        ring_y.arrive(step)
        if step == 3:

            @pl.when(inner)
            def _():
                ring_x.start(0, 2)

        link_and_form(step)
    ring_y.arrive(4)

    @pl.when(inner)
    def _():
        ring_x.start(2)

    link_and_form(4)
    for j in range(ring):
        link[:, cell_columns(j)] = link_cells[j, :, cell]
    scale1 = edge
    scale1[...] = pivot_scale(diags, (d_send, d_recv))
    scale_rows(link, scale1[...], link_scaled)

    hand_link = to_part(link_scaled, sibling, sib, m_send.at[0], m_recv.at[0])
    hand_back = to_part(passed, passed_in, sib, m_send.at[1], m_recv.at[1])
    hand_last = to_part(last, last_in, sib, m_send.at[2], m_recv.at[2])
    hand_fill = to_part(fill_scaled, handed, after, m_send.at[3], m_recv.at[3])
    send_form = to_part(form_cells, update_in, before, m_send.at[4], m_recv.at[4])
    send_square = to_part(square_cells, update_in, before, m_send.at[4], m_recv.at[4])

    @pl.when(outer)
    def _():
        hand_link.start()

    @pl.when(is_odd)
    def _():
        send_form.start()

    def take_left(at, value):
        left_wide[:, at] = x_scaled[:, at].astype(jnp.float32) - value * reciprocal[:, at]

    def round_left():
        left[...] = left_wide[...].astype(jnp.bfloat16)

    def square_cell(step):
        for d in reach[step]:
            put(square_cells, d, dot(left, x_rows(d)))

    def even_result():
        send_form.wait_recv()
        for j in range(ring):
            at = cell_columns(j)
            taken = form_cells[j, :, cell].astype(jnp.float32)
            taken += update_in[j, :, cell].astype(jnp.float32)
            schur_ref[:, at] = sep[:, at] - taken
        link_ref[...] = link[...]

    @pl.when(inner)
    def _():
        diag_part(
            edge2, odd.astype(jnp.float32), [(x_scaled, x_rows(0)), (link_scaled, link)]
        )
        edge_copy(edge2, edge2_in, across, 1).start()
        times(link_scaled, y_all, take_left)
        round_left()
        ring_x.arrive(1)
        hand_link.wait_recv()
        times(sibling, y_all, scaled_into(turned, reciprocal))
        spread(edge2, edge2_in, diags2, across, 1, (d2_send, d2_recv))

        def fill_cell(step):
            for d in reach[step]:
                put(fill_cells, d, dot(turned, x_rows(d)))

        fill_cell(0)
        fill_cell(1)
        ring_x.arrive(2)
        fill_cell(2)
        square_cell(0)
        square_cell(1)
        ring_x.arrive(3)
        pl.semaphore_signal(go, inc=1, device_id={"tm": sib}, device_id_type=MESH)
        fill_cell(3)
        edge2[...] = pivot_scale(diags2, (d2_send, d2_recv))
        ring_x.arrive(4)
        fill_cell(4)
        for j in range(ring):
            turned[:, cell_columns(j)] = fill_cells[j, :, cell]
        scale_rows(turned, edge2[...], fill_scaled)

        @pl.when(role == 1)
        def _():
            hand_fill.start()

        times(fill_scaled, x_all, scaled_into(sibling, reciprocal))
        times_turned(sibling, y_all, scaled_into(passed, scale1))
        hand_back.start()
        square_cell(2)
        square_cell(3)
        square_cell(4)

        @pl.when(role == 2)
        def _():
            send_square.start()
            hand_fill.wait_recv()
            times(handed, x_all, scaled_into(sibling, reciprocal))
            times_turned(sibling, y_all, scaled_into(last, scale1))
            hand_last.start()
            even_result()

        @pl.when(role == 1)
        def _():
            link_ref[...] = turned[...]
            send_square.wait_recv()
            for j in range(ring):
                at = cell_columns(j)
                taken = square_cells[j, :, cell].astype(jnp.float32)
                taken += update_in[j, :, cell].astype(jnp.float32)
                schur_ref[:, at] = sep[:, at] - taken

    order = [d for step in range(ring // 2 + 1) for d in reach[step]]

    def send_cell(d):
        i = order.index(d)
        cells = square_cells.at[near(d)]
        return to_part(cells, update_in.at[near(d)], before, t_send.at[i], t_recv.at[i])

    @pl.when(outer)
    def _():
        times(link_scaled, y_all, take_left)

        @pl.when(role == 0)
        def _():
            even_result()

        pl.semaphore_wait(go, 1)
        ring_x.start()

        def outer_cells(step):
            square_cell(step)

            @pl.when(role == 0)
            def _():
                for d in reach[step]:
                    send_cell(d).start()

        def final_cell(step):
            for d in reach[step]:
                put(final_cells, d, dot(far_left, x_rows(d)))

        ring_x.arrive(1)
        ring_x.arrive(2)
        hand_back.wait_recv()

        def take_more(at, value):
            left_wide[:, at] -= value * reciprocal[:, at]

        times(passed_in, y_all, take_more)
        round_left()
        outer_cells(0)
        outer_cells(1)
        outer_cells(2)
        ring_x.arrive(3)
        outer_cells(3)

        @pl.when(role == 3)
        def _():
            hand_last.wait_recv()
            times(last_in, y_all, scaled_into(far_left, reciprocal))
            for step in range(4):
                final_cell(step)

        ring_x.arrive(4)
        outer_cells(4)

        @pl.when(role == 3)
        def _():
            final_cell(4)
            for j in range(ring):
                at = cell_columns(j)
                schur_ref[:, at] = sep[:, at] - square_cells[j, :, cell].astype(jnp.float32)
                link_ref[:, at] = final_cells[j, :, cell]
            for d in order:
                send_cell(d).wait_recv()

            @pl.when(t != parts - 1)
            def _():
                for j in range(ring):
                    schur_ref[:, cell_columns(j)] -= update_in[j, :, cell].astype(jnp.float32)

    ring_y.drain()
    ring_x.drain()
    for s in range(1, ring):
        spread_copy(diags, s, (d_send, d_recv)).wait_send()

    @pl.when(inner)
    def _():
        hand_back.wait_send()
        for s in range(1, ring):
            spread_copy(diags2, s, (d2_send, d2_recv)).wait_send()

    @pl.when(outer)
    def _():
        hand_link.wait_send()

    @pl.when(is_odd)
    def _():
        send_form.wait_send()

    @pl.when(role == 0)
    def _():
        for d in order:
            send_cell(d).wait_send()

    @pl.when(role == 1)
    def _():
        hand_fill.wait_send()

    @pl.when(role == 2)
    def _():
        send_square.wait_send()
        hand_last.wait_send()


def solution(mesh):
    ring, parts = mesh.shape["space"], mesh.shape["tm"]

    def on_device(sep_block, own_couple, prev_couple, inner_diag):
        rows, width = sep_block.shape[1:]

        def block(kind, *lead):
            return pltpu.VMEM((*lead, rows, width), kind)

        def full(*lead):
            return pltpu.VMEM((*lead, width, width), jnp.bfloat16)

        line = pltpu.VMEM((1, width), jnp.float32)
        lines = pltpu.VMEM((ring, 1, width), jnp.float32)
        half = jnp.bfloat16
        dma = lambda count: pltpu.SemaphoreType.DMA((count,))
        cells = pltpu.VMEM((ring, rows, -(-rows // 128) * 128), half)
        schur, link = pl.pallas_call(
            functools.partial(kernel, ring, parts),
            out_shape=(
                jax.ShapeDtypeStruct((rows, width), jnp.float32),
                jax.ShapeDtypeStruct((rows, width), half),
            ),
            in_specs=[pl.BlockSpec(memory_space=pl.ANY)] * 3
            + [pl.BlockSpec(memory_space=pltpu.VMEM)],
            out_specs=(pl.BlockSpec(memory_space=pltpu.VMEM),) * 2,
            scratch_shapes=[
                block(jnp.float32), full(2), block(half, 2), *[block(half)] * 10,
                block(half), block(jnp.float32), block(half), *[cells] * 6,
                line, line, line, lines, line, line, lines,
                dma(3), dma(2 * ring), dma(2 * ring), dma(4 * ring), dma(4 * ring),
                dma(ring - 1), dma(ring - 1), dma(ring - 1), dma(ring - 1),
                dma(2), dma(2), dma(5), dma(5), dma(ring), dma(ring), pltpu.SemaphoreType.REGULAR,
            ],
            compiler_params=pltpu.CompilerParams(
                collective_id=0, has_side_effects=True, vmem_limit_bytes=56 * 2**20
            ),
            cost_estimate=pl.CostEstimate(
                flops=7 * 2 * rows * width * width, bytes_accessed=10 * rows * width, transcendentals=0
            ),
        )(sep_block[0], own_couple[0], prev_couple[0], inner_diag)
        return schur[None], link[None]

    placed = (P("tm", "space", None), P("tm", "space", None), P("tm", "space", None), P("tm", None))
    return jax.shard_map(
        on_device,
        mesh=mesh,
        in_specs=placed,
        out_specs=(P("tm", "space", None), P("tm", "space", None)),
        check_vma=False,
    )
```

```python
import functools

import jax
import jax.numpy as jnp
from jax import lax
from jax.experimental import pallas as pl
from jax.experimental.pallas import tpu as pltpu
from jax.sharding import PartitionSpec as P

MESH = pl.DeviceIdType.MESH
OWN, PREV = 0, 1


def kernel(
    ring, parts, sep_hbm, own_hbm, prev_hbm, diag_ref, schur_ref, link_ref,
    sep, pair, scaled, link, link_scaled, sibling, turned, fill_scaled, handed,
    passed, passed_in, last, last_in, left, left_wide, far_left,
    link_cells, form_cells, fill_cells, square_cells, final_cells, update_in,
    reciprocal, edge, edge_in, diags, edge2, edge2_in, diags2,
    load_sem, y_send, y_recv, x_send, x_recv,
    d_send, d_recv, d2_send, d2_recv, e_send, e_recv, m_send, m_recv, t_send, t_recv, go,
):
    rows, width = sep.shape
    chunk = 16
    tile = 512
    z = lax.axis_index("space")
    t = lax.axis_index("tm")
    odd = lax.rem(t, 2)
    role = lax.rem(t, 4)
    is_odd = odd == 1
    inner = jnp.logical_or(role == 1, role == 2)
    outer = jnp.logical_not(inner)
    sib = t + 1 - 2 * odd
    across = lax.rem(t + 2 * odd - 1 + parts, parts)
    before = lax.rem(t + parts - 1, parts)
    after = lax.rem(t + 1, parts)
    first, second = 1 - odd, odd

    barrier = pltpu.get_barrier_semaphore()
    for k in range(1, ring):
        pl.semaphore_signal(
            barrier, inc=1, device_id={"space": lax.rem(z + k, ring)}, device_id_type=MESH
        )
    for peer in (before, after):
        pl.semaphore_signal(barrier, inc=1, device_id={"tm": peer}, device_id_type=MESH)

    def near(d):
        return lax.rem(z + d + ring, ring)

    def row_slice(d):
        return pl.ds(pl.multiple_of(near(d) * rows, rows), rows)

    def cell_columns(j):
        return slice(j * rows, (j + 1) * rows)

    loads = [
        pltpu.make_async_copy(own_hbm, pair.at[OWN, row_slice(0)], load_sem.at[0]),
        pltpu.make_async_copy(prev_hbm, pair.at[PREV, row_slice(0)], load_sem.at[1]),
        pltpu.make_async_copy(sep_hbm, sep, load_sem.at[2]),
    ]
    for load in loads:
        load.start()
    for load in loads:
        load.wait()
    pl.semaphore_wait(barrier, ring + 1)

    def along(src, dst, way, send_sem, recv_sem):
        return pltpu.make_async_remote_copy(
            src_ref=src, dst_ref=dst, send_sem=send_sem, recv_sem=recv_sem,
            device_id={"space": near(way)}, device_id_type=MESH,
        )

    def to_part(src, dst, peer, send_sem, recv_sem):
        return pltpu.make_async_remote_copy(
            src_ref=src, dst_ref=dst, send_sem=send_sem, recv_sem=recv_sem,
            device_id={"tm": peer}, device_id_type=MESH,
        )

    class Ring:
        def __init__(self, buf, pieces, send_sem, recv_sem):
            size = rows // pieces
            self.streams = []
            for i in range(pieces):
                long_way = 1 if i % 2 == 0 else -1
                self.streams.append((buf, i * size, size, long_way, ring // 2))
                self.streams.append((buf, i * size, size, -long_way, ring // 2 - 1))
            self.sems = send_sem, recv_sem

        def at(self, s, step):
            buf, offset, count, way, _ = self.streams[s]
            at = s * (ring // 2) + step - 1
            slot = near(-way * (step - 1))
            piece = buf.at[pl.ds(pl.multiple_of(slot * rows + offset, chunk), count)]
            return along(piece, piece, way, self.sems[0].at[at], self.sems[1].at[at])

        def start(self, begin=0, end=None):
            for s in range(len(self.streams))[begin:end]:
                self.at(s, 1).start()

        def arrive(self, step):
            for s, stream in enumerate(self.streams):
                if step <= stream[4]:
                    self.at(s, step).wait_recv()
                    if step < stream[4]:
                        self.at(s, step + 1).start()

        def drain(self):
            for s, stream in enumerate(self.streams):
                for step in range(1, stream[4] + 1):
                    self.at(s, step).wait_send()

    x_all = pair.at[first]
    y_all = pair.at[second]
    ring_y = Ring(y_all, 2, y_send, y_recv)
    ring_x = Ring(x_all, 4, x_send, x_recv)
    ring_y.start()

    def diag_part(out, sep_factor, terms):
        out[...] = jnp.zeros_like(out)

        @pl.loop(0, rows // chunk)
        def _(i):
            at = pl.multiple_of(i * chunk, chunk)
            total = jnp.zeros((chunk, 1), jnp.float32)
            for left_rows, right_rows in terms:
                total += jnp.sum(
                    left_rows[pl.ds(at, chunk), :].astype(jnp.float32)
                    * right_rows[pl.ds(at, chunk), :].astype(jnp.float32),
                    axis=1, keepdims=True,
                )
            spot = lax.broadcasted_iota(jnp.int32, (chunk, width), 1) == (
                lax.broadcasted_iota(jnp.int32, (chunk, width), 0) + (z * rows + at)
            )
            values = sep[pl.ds(at, chunk), :] * sep_factor - total
            out[...] += jnp.sum(jnp.where(spot, values, 0.0), axis=0, keepdims=True)

    def edge_copy(edge, edge_in, peer, k):
        return to_part(edge, edge_in, peer, e_send.at[k], e_recv.at[k])

    def spread_copy(diags, s, sems):
        return along(diags.at[z], diags.at[z], s, sems[0].at[s - 1], sems[1].at[s - 1])

    def spread(edge, edge_in, diags, peer, k, sems):
        edge_copy(edge, edge_in, peer, k).wait()
        diags[z] = edge[...] + edge_in[...]
        for s in range(1, ring):
            spread_copy(diags, s, sems).start()

    def pivot_scale(diags, sems):
        for s in range(1, ring):
            spread_copy(diags, s, sems).wait_recv()
        values = diags[0]
        for s in range(1, ring):
            values += diags[s]
        return (1.0 / jnp.maximum(values, 1.0)).astype(jnp.bfloat16).astype(jnp.float32)

    def scale_rows(source, factors, out):
        @pl.loop(0, rows // chunk)
        def _(i):
            at = pl.ds(pl.multiple_of(i * chunk, chunk), chunk)
            out[at, :] = (source[at, :].astype(jnp.float32) * factors).astype(jnp.bfloat16)

    def dot(left_rows, right_rows):
        return lax.dot_general(
            left_rows[...], right_rows[...], (((1,), (1,)), ((), ())),
            preferred_element_type=jnp.float32,
        )

    def times(left_rows, matrix, take):
        @pl.loop(0, width // tile)
        def _(j):
            at = pl.ds(pl.multiple_of(j * tile, tile), tile)
            take(at, jnp.dot(left_rows[...], matrix[:, at], preferred_element_type=jnp.float32))

    def times_turned(left_rows, matrix, take):
        @pl.loop(0, width // tile)
        def _(j):
            at = pl.ds(pl.multiple_of(j * tile, tile), tile)
            take(at, dot(left_rows, matrix.at[at]))

    def scaled_into(out, factors):
        def take(at, value):
            out[:, at] = (value * factors[:, at]).astype(jnp.bfloat16)

        return take

    cell = slice(0, rows)

    def put(cells, d, value):
        cells[near(d), :, cell] = value.astype(jnp.bfloat16)

    def x_rows(d):
        return x_all.at[row_slice(d)]

    def y_rows(d):
        return y_all.at[row_slice(d)]

    reach = {0: (0,), 4: (ring // 2,)}
    for step in range(1, ring // 2):
        reach[step] = (-step, step)

    reciprocal[...] = 1.0 / diag_ref[...]
    x_scaled, y_scaled = scaled.at[0], scaled.at[1]
    scale_rows(y_rows(0), reciprocal[...], y_scaled)
    scale_rows(x_rows(0), reciprocal[...], x_scaled)
    diag_part(edge, (1 - odd).astype(jnp.float32), [(y_scaled, y_rows(0))])
    edge_copy(edge, edge_in, sib, 0).start()
    spread(edge, edge_in, diags, sib, 0, (d_send, d_recv))

    sign = jnp.where(t == 0, 0.0, -1.0)

    def link_and_form(step):
        for d in reach[step]:
            put(link_cells, d, dot(x_scaled, y_rows(d)) * sign)
            put(form_cells, d, dot(y_scaled, y_rows(d)))

    link_and_form(0)
    for step in (1, 2, 3):
        ring_y.arrive(step)
        if step == 3:

            @pl.when(inner)
            def _():
                ring_x.start(0, 2)

        link_and_form(step)
    ring_y.arrive(4)

    @pl.when(inner)
    def _():
        ring_x.start(2)

    link_and_form(4)
    for j in range(ring):
        link[:, cell_columns(j)] = link_cells[j, :, cell]
    scale1 = edge
    scale1[...] = pivot_scale(diags, (d_send, d_recv))
    scale_rows(link, scale1[...], link_scaled)

    hand_link = to_part(link_scaled, sibling, sib, m_send.at[0], m_recv.at[0])
    hand_back = to_part(passed, passed_in, sib, m_send.at[1], m_recv.at[1])
    hand_last = to_part(last, last_in, sib, m_send.at[2], m_recv.at[2])
    hand_fill = to_part(fill_scaled, handed, after, m_send.at[3], m_recv.at[3])
    send_form = to_part(form_cells, update_in, before, m_send.at[4], m_recv.at[4])
    send_square = to_part(square_cells, update_in, before, m_send.at[4], m_recv.at[4])

    @pl.when(outer)
    def _():
        hand_link.start()

    @pl.when(is_odd)
    def _():
        send_form.start()

    def take_left(at, value):
        left_wide[:, at] = x_scaled[:, at].astype(jnp.float32) - value * reciprocal[:, at]

    def round_left():
        left[...] = left_wide[...].astype(jnp.bfloat16)

    def square_cell(step):
        for d in reach[step]:
            put(square_cells, d, dot(left, x_rows(d)))

    def even_result():
        send_form.wait_recv()
        for j in range(ring):
            at = cell_columns(j)
            taken = form_cells[j, :, cell].astype(jnp.float32)
            taken += update_in[j, :, cell].astype(jnp.float32)
            schur_ref[:, at] = taken.astype(jnp.bfloat16)
        link_ref[...] = link[...]

    @pl.when(inner)
    def _():
        diag_part(
            edge2, odd.astype(jnp.float32), [(x_scaled, x_rows(0)), (link_scaled, link)]
        )
        edge_copy(edge2, edge2_in, across, 1).start()
        times(link_scaled, y_all, take_left)
        round_left()
        ring_x.arrive(1)
        hand_link.wait_recv()
        times(sibling, y_all, scaled_into(turned, reciprocal))
        spread(edge2, edge2_in, diags2, across, 1, (d2_send, d2_recv))

        def fill_cell(step):
            for d in reach[step]:
                put(fill_cells, d, dot(turned, x_rows(d)))

        fill_cell(0)
        fill_cell(1)
        ring_x.arrive(2)
        fill_cell(2)
        square_cell(0)
        square_cell(1)
        ring_x.arrive(3)
        pl.semaphore_signal(go, inc=1, device_id={"tm": sib}, device_id_type=MESH)
        fill_cell(3)
        edge2[...] = pivot_scale(diags2, (d2_send, d2_recv))
        ring_x.arrive(4)
        fill_cell(4)
        for j in range(ring):
            turned[:, cell_columns(j)] = fill_cells[j, :, cell]
        scale_rows(turned, edge2[...], fill_scaled)

        @pl.when(role == 1)
        def _():
            hand_fill.start()

        times(fill_scaled, x_all, scaled_into(sibling, reciprocal))
        times_turned(sibling, y_all, scaled_into(passed, scale1))
        hand_back.start()
        square_cell(2)
        square_cell(3)
        square_cell(4)

        @pl.when(role == 2)
        def _():
            send_square.start()
            hand_fill.wait_recv()
            times(handed, x_all, scaled_into(sibling, reciprocal))
            times_turned(sibling, y_all, scaled_into(last, scale1))
            hand_last.start()
            even_result()

        @pl.when(role == 1)
        def _():
            link_ref[...] = turned[...]
            send_square.wait_recv()
            for j in range(ring):
                at = cell_columns(j)
                taken = square_cells[j, :, cell].astype(jnp.float32)
                taken += update_in[j, :, cell].astype(jnp.float32)
                schur_ref[:, at] = taken.astype(jnp.bfloat16)

    order = [d for step in range(ring // 2 + 1) for d in reach[step]]

    def send_cell(d):
        i = order.index(d)
        cells = square_cells.at[near(d)]
        return to_part(cells, update_in.at[near(d)], before, t_send.at[i], t_recv.at[i])

    @pl.when(outer)
    def _():
        times(link_scaled, y_all, take_left)

        @pl.when(role == 0)
        def _():
            even_result()

        pl.semaphore_wait(go, 1)
        ring_x.start()

        def outer_cells(step):
            square_cell(step)

            @pl.when(role == 0)
            def _():
                for d in reach[step]:
                    send_cell(d).start()

        def final_cell(step):
            for d in reach[step]:
                put(final_cells, d, dot(far_left, x_rows(d)))

        ring_x.arrive(1)
        ring_x.arrive(2)
        hand_back.wait_recv()

        def take_more(at, value):
            left_wide[:, at] -= value * reciprocal[:, at]

        times(passed_in, y_all, take_more)
        round_left()
        outer_cells(0)
        outer_cells(1)
        outer_cells(2)
        ring_x.arrive(3)
        outer_cells(3)

        @pl.when(role == 3)
        def _():
            hand_last.wait_recv()
            times(last_in, y_all, scaled_into(far_left, reciprocal))
            for step in range(4):
                final_cell(step)

        ring_x.arrive(4)
        outer_cells(4)

        @pl.when(role == 3)
        def _():
            final_cell(4)
            for j in range(ring):
                at = cell_columns(j)
                schur_ref[:, at] = square_cells[j, :, cell]
                link_ref[:, at] = final_cells[j, :, cell]
            for d in order:
                send_cell(d).wait_recv()

            @pl.when(t != parts - 1)
            def _():
                for j in range(ring):
                    at = cell_columns(j)
                    taken = square_cells[j, :, cell].astype(jnp.float32)
                    taken += update_in[j, :, cell].astype(jnp.float32)
                    schur_ref[:, at] = taken.astype(jnp.bfloat16)

    ring_y.drain()
    ring_x.drain()
    for s in range(1, ring):
        spread_copy(diags, s, (d_send, d_recv)).wait_send()

    @pl.when(inner)
    def _():
        hand_back.wait_send()
        for s in range(1, ring):
            spread_copy(diags2, s, (d2_send, d2_recv)).wait_send()

    @pl.when(outer)
    def _():
        hand_link.wait_send()

    @pl.when(is_odd)
    def _():
        send_form.wait_send()

    @pl.when(role == 0)
    def _():
        for d in order:
            send_cell(d).wait_send()

    @pl.when(role == 1)
    def _():
        hand_fill.wait_send()

    @pl.when(role == 2)
    def _():
        send_square.wait_send()
        hand_last.wait_send()


def finish(sep_in, taken_in, link_in, schur_out, link_out, sep, taken, link, sems):
    count = 4
    step = sep_in.shape[0] // count
    slabs = [pl.ds(i * step, step) for i in range(count)]
    loads, stores = [], []
    for i, at in enumerate(slabs):
        for k, (src, dst) in enumerate(((sep_in, sep), (taken_in, taken), (link_in, link))):
            copy = pltpu.make_async_copy(src.at[at], dst.at[at], sems.at[k, i])
            copy.start()
            loads.append(copy)
    for i, at in enumerate(slabs):
        for k in range(3):
            loads[3 * i + k].wait()
        sep[at, :] -= taken[at, :].astype(jnp.float32)
        for k, (src, dst) in enumerate(((sep, schur_out), (link, link_out))):
            copy = pltpu.make_async_copy(src.at[at], dst.at[at], sems.at[3 + k, i])
            copy.start()
            stores.append(copy)
    for copy in stores:
        copy.wait()


def solution(mesh):
    ring, parts = mesh.shape["space"], mesh.shape["tm"]

    def on_device(sep_block, own_couple, prev_couple, inner_diag):
        rows, width = sep_block.shape[1:]

        def block(kind, *lead):
            return pltpu.VMEM((*lead, rows, width), kind)

        def full(*lead):
            return pltpu.VMEM((*lead, width, width), jnp.bfloat16)

        line = pltpu.VMEM((1, width), jnp.float32)
        lines = pltpu.VMEM((ring, 1, width), jnp.float32)
        half = jnp.bfloat16
        dma = lambda count: pltpu.SemaphoreType.DMA((count,))
        cells = pltpu.VMEM((ring, rows, -(-rows // 128) * 128), half)
        taken, link = pl.pallas_call(
            functools.partial(kernel, ring, parts),
            out_shape=(
                jax.ShapeDtypeStruct((rows, width), half),
                jax.ShapeDtypeStruct((rows, width), half),
            ),
            in_specs=[pl.BlockSpec(memory_space=pl.ANY)] * 3
            + [pl.BlockSpec(memory_space=pltpu.VMEM)],
            out_specs=(pl.BlockSpec(memory_space=pltpu.VMEM),) * 2,
            scratch_shapes=[
                block(jnp.float32), full(2), block(half, 2), *[block(half)] * 10,
                block(half), block(jnp.float32), block(half), *[cells] * 6,
                line, line, line, lines, line, line, lines,
                dma(3), dma(2 * ring), dma(2 * ring), dma(4 * ring), dma(4 * ring),
                dma(ring - 1), dma(ring - 1), dma(ring - 1), dma(ring - 1),
                dma(2), dma(2), dma(5), dma(5), dma(ring), dma(ring), pltpu.SemaphoreType.REGULAR,
            ],
            compiler_params=pltpu.CompilerParams(
                collective_id=0, has_side_effects=True, vmem_limit_bytes=63 * 2**20
            ),
            cost_estimate=pl.CostEstimate(
                flops=7 * 2 * rows * width * width, bytes_accessed=10 * rows * width, transcendentals=0
            ),
        )(sep_block[0], own_couple[0], prev_couple[0], inner_diag)
        schur, link = pl.pallas_call(
            finish,
            out_shape=(
                jax.ShapeDtypeStruct((rows, width), jnp.float32),
                jax.ShapeDtypeStruct((rows, width), half),
            ),
            in_specs=[pl.BlockSpec(memory_space=pl.ANY)] * 3,
            out_specs=(pl.BlockSpec(memory_space=pl.ANY),) * 2,
            scratch_shapes=[
                block(jnp.float32), block(half), block(half), pltpu.SemaphoreType.DMA((5, 4))
            ],
            compiler_params=pltpu.CompilerParams(vmem_limit_bytes=60 * 2**20),
        )(sep_block[0], taken, link)
        return schur[None], link[None]

    placed = (P("tm", "space", None), P("tm", "space", None), P("tm", "space", None), P("tm", None))
    return jax.shard_map(
        on_device,
        mesh=mesh,
        in_specs=placed,
        out_specs=(P("tm", "space", None), P("tm", "space", None)),
        check_vma=False,
    )
```

```python
import functools

import jax
import jax.numpy as jnp
from jax import lax
from jax.experimental import pallas as pl
from jax.experimental.pallas import tpu as pltpu
from jax.sharding import PartitionSpec as P

MESH = pl.DeviceIdType.MESH
OWN, PREV = 0, 1


def kernel(
    ring, parts, sep_hbm, own_hbm, prev_hbm, diag_ref, schur_ref, link_ref,
    sep, pair, scaled, link, link_scaled, sibling, turned, fill_scaled, handed,
    passed, passed_in, last, last_in, left, left_wide, far_left,
    link_cells, form_cells, fill_cells, square_cells, final_cells, update_in,
    reciprocal, edge, edge_in, diags, edge2, edge2_in, diags2,
    load_sem, y_send, y_recv, x_send, x_recv,
    d_send, d_recv, d2_send, d2_recv, e_send, e_recv, m_send, m_recv, t_send, t_recv, go,
):
    rows, width = sep.shape
    chunk = 16
    tile = 512
    z = lax.axis_index("space")
    t = lax.axis_index("tm")
    odd = lax.rem(t, 2)
    role = lax.rem(t, 4)
    is_odd = odd == 1
    inner = jnp.logical_or(role == 1, role == 2)
    outer = jnp.logical_not(inner)
    sib = t + 1 - 2 * odd
    across = lax.rem(t + 2 * odd - 1 + parts, parts)
    before = lax.rem(t + parts - 1, parts)
    after = lax.rem(t + 1, parts)
    first, second = 1 - odd, odd

    barrier = pltpu.get_barrier_semaphore()
    for k in range(1, ring):
        pl.semaphore_signal(
            barrier, inc=1, device_id={"space": lax.rem(z + k, ring)}, device_id_type=MESH
        )
    for peer in (before, after):
        pl.semaphore_signal(barrier, inc=1, device_id={"tm": peer}, device_id_type=MESH)

    def near(d):
        return lax.rem(z + d + ring, ring)

    def row_slice(d):
        return pl.ds(pl.multiple_of(near(d) * rows, rows), rows)

    def cell_columns(j):
        return slice(j * rows, (j + 1) * rows)

    loads = [
        pltpu.make_async_copy(own_hbm, pair.at[OWN, row_slice(0)], load_sem.at[0]),
        pltpu.make_async_copy(prev_hbm, pair.at[PREV, row_slice(0)], load_sem.at[1]),
        pltpu.make_async_copy(sep_hbm, sep, load_sem.at[2]),
    ]
    for load in loads:
        load.start()
    for load in loads:
        load.wait()
    pl.semaphore_wait(barrier, ring + 1)

    def along(src, dst, way, send_sem, recv_sem):
        return pltpu.make_async_remote_copy(
            src_ref=src, dst_ref=dst, send_sem=send_sem, recv_sem=recv_sem,
            device_id={"space": near(way)}, device_id_type=MESH,
        )

    def to_part(src, dst, peer, send_sem, recv_sem):
        return pltpu.make_async_remote_copy(
            src_ref=src, dst_ref=dst, send_sem=send_sem, recv_sem=recv_sem,
            device_id={"tm": peer}, device_id_type=MESH,
        )

    class Ring:
        def __init__(self, buf, pieces, send_sem, recv_sem):
            size = rows // pieces
            self.streams = []
            for i in range(pieces):
                long_way = 1 if i % 2 == 0 else -1
                self.streams.append((buf, i * size, size, long_way, ring // 2))
                self.streams.append((buf, i * size, size, -long_way, ring // 2 - 1))
            self.sems = send_sem, recv_sem

        def at(self, s, step):
            buf, offset, count, way, _ = self.streams[s]
            at = s * (ring // 2) + step - 1
            slot = near(-way * (step - 1))
            piece = buf.at[pl.ds(pl.multiple_of(slot * rows + offset, chunk), count)]
            return along(piece, piece, way, self.sems[0].at[at], self.sems[1].at[at])

        def start(self, begin=0, end=None):
            for s in range(len(self.streams))[begin:end]:
                self.at(s, 1).start()

        def arrive(self, step):
            for s, stream in enumerate(self.streams):
                if step <= stream[4]:
                    self.at(s, step).wait_recv()
                    if step < stream[4]:
                        self.at(s, step + 1).start()

        def drain(self):
            for s, stream in enumerate(self.streams):
                for step in range(1, stream[4] + 1):
                    self.at(s, step).wait_send()

    x_all = pair.at[first]
    y_all = pair.at[second]
    ring_y = Ring(y_all, 2, y_send, y_recv)
    ring_x = Ring(x_all, 4, x_send, x_recv)
    ring_y.start()

    def diag_part(out, sep_factor, terms):
        out[...] = jnp.zeros_like(out)

        @pl.loop(0, rows // chunk)
        def _(i):
            at = pl.multiple_of(i * chunk, chunk)
            total = jnp.zeros((chunk, 1), jnp.float32)
            for left_rows, right_rows in terms:
                total += jnp.sum(
                    left_rows[pl.ds(at, chunk), :].astype(jnp.float32)
                    * right_rows[pl.ds(at, chunk), :].astype(jnp.float32),
                    axis=1, keepdims=True,
                )
            spot = lax.broadcasted_iota(jnp.int32, (chunk, width), 1) == (
                lax.broadcasted_iota(jnp.int32, (chunk, width), 0) + (z * rows + at)
            )
            values = sep[pl.ds(at, chunk), :] * sep_factor - total
            out[...] += jnp.sum(jnp.where(spot, values, 0.0), axis=0, keepdims=True)

    def edge_copy(edge, edge_in, peer, k):
        return to_part(edge, edge_in, peer, e_send.at[k], e_recv.at[k])

    span = 2 * rows
    my_span = pl.ds(pl.multiple_of(lax.div(z, 2) * span, span), span)

    def spread_copy(diags, s, sems):
        mine = diags.at[z, :, my_span]
        return along(mine, mine, s, sems[0].at[s - 1], sems[1].at[s - 1])

    def spread(edge, edge_in, diags, peer, k, sems):
        edge_copy(edge, edge_in, peer, k).wait()
        diags[z] = edge[...] + edge_in[...]
        for s in range(1, ring):
            spread_copy(diags, s, sems).start()

    def pivot_scale(diags, sems, out):
        for s in range(1, ring):
            spread_copy(diags, s, sems).wait_recv()
        for k in range(ring // 2):
            at = slice(k * span, (k + 1) * span)
            values = diags[2 * k, :, at] + diags[2 * k + 1, :, at]
            scale = (1.0 / jnp.maximum(values, 1.0)).astype(jnp.bfloat16)
            out[:, at] = scale.astype(jnp.float32)

    def scale_rows(source, factors, out):
        @pl.loop(0, rows // chunk)
        def _(i):
            at = pl.ds(pl.multiple_of(i * chunk, chunk), chunk)
            out[at, :] = (source[at, :].astype(jnp.float32) * factors).astype(jnp.bfloat16)

    def dot(left_rows, right_rows):
        return lax.dot_general(
            left_rows[...], right_rows[...], (((1,), (1,)), ((), ())),
            preferred_element_type=jnp.float32,
        )

    def times(left_rows, matrix, take):
        @pl.loop(0, width // tile)
        def _(j):
            at = pl.ds(pl.multiple_of(j * tile, tile), tile)
            take(at, jnp.dot(left_rows[...], matrix[:, at], preferred_element_type=jnp.float32))

    def times_turned(left_rows, matrix, take):
        @pl.loop(0, width // tile)
        def _(j):
            at = pl.ds(pl.multiple_of(j * tile, tile), tile)
            take(at, dot(left_rows, matrix.at[at]))

    def scaled_into(out, factors):
        def take(at, value):
            out[:, at] = (value * factors[:, at]).astype(jnp.bfloat16)

        return take

    cell = slice(0, rows)

    def put(cells, d, value):
        cells[near(d), :, cell] = value.astype(jnp.bfloat16)

    def x_rows(d):
        return x_all.at[row_slice(d)]

    def y_rows(d):
        return y_all.at[row_slice(d)]

    reach = {0: (0,), 4: (ring // 2,)}
    for step in range(1, ring // 2):
        reach[step] = (-step, step)

    reciprocal[...] = 1.0 / diag_ref[...]
    x_scaled, y_scaled = scaled.at[0], scaled.at[1]
    scale_rows(y_rows(0), reciprocal[...], y_scaled)
    scale_rows(x_rows(0), reciprocal[...], x_scaled)
    diag_part(edge, (1 - odd).astype(jnp.float32), [(y_scaled, y_rows(0))])
    edge_copy(edge, edge_in, sib, 0).start()
    spread(edge, edge_in, diags, sib, 0, (d_send, d_recv))

    sign = jnp.where(t == 0, 0.0, -1.0)

    def link_and_form(step):
        for d in reach[step]:
            put(link_cells, d, dot(x_scaled, y_rows(d)) * sign)
            put(form_cells, d, dot(y_scaled, y_rows(d)))

    link_and_form(0)
    for step in (1, 2, 3):
        ring_y.arrive(step)
        if step == 3:

            @pl.when(inner)
            def _():
                ring_x.start(0, 2)

        link_and_form(step)
    ring_y.arrive(4)

    @pl.when(inner)
    def _():
        ring_x.start(2)

    link_and_form(4)
    for j in range(ring):
        link[:, cell_columns(j)] = link_cells[j, :, cell]
    scale1 = edge
    pivot_scale(diags, (d_send, d_recv), scale1)
    scale_rows(link, scale1[...], link_scaled)

    hand_link = to_part(link_scaled, sibling, sib, m_send.at[0], m_recv.at[0])
    hand_back = to_part(passed, passed_in, sib, m_send.at[1], m_recv.at[1])
    hand_last = to_part(last, last_in, sib, m_send.at[2], m_recv.at[2])
    hand_fill = to_part(fill_scaled, handed, after, m_send.at[3], m_recv.at[3])
    send_form = to_part(form_cells, update_in, before, m_send.at[4], m_recv.at[4])
    send_square = to_part(square_cells, update_in, before, m_send.at[4], m_recv.at[4])

    @pl.when(outer)
    def _():
        hand_link.start()

    @pl.when(is_odd)
    def _():
        send_form.start()

    def take_left(at, value):
        left_wide[:, at] = x_scaled[:, at].astype(jnp.float32) - value * reciprocal[:, at]

    def round_left():
        left[...] = left_wide[...].astype(jnp.bfloat16)

    def square_cell(step):
        for d in reach[step]:
            put(square_cells, d, dot(left, x_rows(d)))

    def even_result():
        send_form.wait_recv()
        for j in range(ring):
            at = cell_columns(j)
            taken = form_cells[j, :, cell].astype(jnp.float32)
            taken += update_in[j, :, cell].astype(jnp.float32)
            schur_ref[:, at] = taken.astype(jnp.bfloat16)
        link_ref[...] = link[...]

    @pl.when(inner)
    def _():
        diag_part(
            edge2, odd.astype(jnp.float32), [(x_scaled, x_rows(0)), (link_scaled, link)]
        )
        edge_copy(edge2, edge2_in, across, 1).start()
        times(link_scaled, y_all, take_left)
        round_left()
        ring_x.arrive(1)
        hand_link.wait_recv()
        times(sibling, y_all, scaled_into(turned, reciprocal))
        spread(edge2, edge2_in, diags2, across, 1, (d2_send, d2_recv))

        def fill_cell(step):
            for d in reach[step]:
                put(fill_cells, d, dot(turned, x_rows(d)))

        fill_cell(0)
        fill_cell(1)
        ring_x.arrive(2)
        fill_cell(2)
        square_cell(0)
        square_cell(1)
        ring_x.arrive(3)
        pl.semaphore_signal(go, inc=1, device_id={"tm": sib}, device_id_type=MESH)
        fill_cell(3)
        pivot_scale(diags2, (d2_send, d2_recv), edge2)
        ring_x.arrive(4)
        fill_cell(4)
        for j in range(ring):
            turned[:, cell_columns(j)] = fill_cells[j, :, cell]
        scale_rows(turned, edge2[...], fill_scaled)

        @pl.when(role == 1)
        def _():
            hand_fill.start()

        times(fill_scaled, x_all, scaled_into(sibling, reciprocal))
        times_turned(sibling, y_all, scaled_into(passed, scale1))
        hand_back.start()
        square_cell(2)
        square_cell(3)
        square_cell(4)

        @pl.when(role == 2)
        def _():
            send_square.start()
            hand_fill.wait_recv()
            times(handed, x_all, scaled_into(sibling, reciprocal))
            times_turned(sibling, y_all, scaled_into(last, scale1))
            hand_last.start()
            even_result()

        @pl.when(role == 1)
        def _():
            link_ref[...] = turned[...]
            send_square.wait_recv()
            for j in range(ring):
                at = cell_columns(j)
                taken = square_cells[j, :, cell].astype(jnp.float32)
                taken += update_in[j, :, cell].astype(jnp.float32)
                schur_ref[:, at] = taken.astype(jnp.bfloat16)

    order = [d for step in range(ring // 2 + 1) for d in reach[step]]

    def send_cell(d):
        i = order.index(d)
        cells = square_cells.at[near(d)]
        return to_part(cells, update_in.at[near(d)], before, t_send.at[i], t_recv.at[i])

    @pl.when(outer)
    def _():
        times(link_scaled, y_all, take_left)

        @pl.when(role == 0)
        def _():
            even_result()

        pl.semaphore_wait(go, 1)
        ring_x.start()

        def outer_cells(step):
            square_cell(step)

            @pl.when(role == 0)
            def _():
                for d in reach[step]:
                    send_cell(d).start()

        def final_cell(step):
            for d in reach[step]:
                put(final_cells, d, dot(far_left, x_rows(d)))

        ring_x.arrive(1)
        ring_x.arrive(2)
        hand_back.wait_recv()

        def take_more(at, value):
            left_wide[:, at] -= value * reciprocal[:, at]

        times(passed_in, y_all, take_more)
        round_left()
        outer_cells(0)
        outer_cells(1)
        outer_cells(2)
        ring_x.arrive(3)
        outer_cells(3)

        @pl.when(role == 3)
        def _():
            hand_last.wait_recv()
            times(last_in, y_all, scaled_into(far_left, reciprocal))
            for step in range(4):
                final_cell(step)

        ring_x.arrive(4)
        outer_cells(4)

        @pl.when(role == 3)
        def _():
            final_cell(4)
            for j in range(ring):
                at = cell_columns(j)
                schur_ref[:, at] = square_cells[j, :, cell]
                link_ref[:, at] = final_cells[j, :, cell]
            for d in order:
                send_cell(d).wait_recv()

            @pl.when(t != parts - 1)
            def _():
                for j in range(ring):
                    at = cell_columns(j)
                    taken = square_cells[j, :, cell].astype(jnp.float32)
                    taken += update_in[j, :, cell].astype(jnp.float32)
                    schur_ref[:, at] = taken.astype(jnp.bfloat16)

    ring_y.drain()
    ring_x.drain()
    for s in range(1, ring):
        spread_copy(diags, s, (d_send, d_recv)).wait_send()

    @pl.when(inner)
    def _():
        hand_back.wait_send()
        for s in range(1, ring):
            spread_copy(diags2, s, (d2_send, d2_recv)).wait_send()

    @pl.when(outer)
    def _():
        hand_link.wait_send()

    @pl.when(is_odd)
    def _():
        send_form.wait_send()

    @pl.when(role == 0)
    def _():
        for d in order:
            send_cell(d).wait_send()

    @pl.when(role == 1)
    def _():
        hand_fill.wait_send()

    @pl.when(role == 2)
    def _():
        send_square.wait_send()
        hand_last.wait_send()


def finish(sep_in, taken_in, link_in, schur_out, link_out, sep, taken, link, sems):
    count = 4
    step = sep_in.shape[0] // count
    slabs = [pl.ds(i * step, step) for i in range(count)]
    loads, stores = [], []
    for i, at in enumerate(slabs):
        for k, (src, dst) in enumerate(((sep_in, sep), (taken_in, taken), (link_in, link))):
            copy = pltpu.make_async_copy(src.at[at], dst.at[at], sems.at[k, i])
            copy.start()
            loads.append(copy)
    for i, at in enumerate(slabs):
        for k in range(3):
            loads[3 * i + k].wait()
        sep[at, :] -= taken[at, :].astype(jnp.float32)
        for k, (src, dst) in enumerate(((sep, schur_out), (link, link_out))):
            copy = pltpu.make_async_copy(src.at[at], dst.at[at], sems.at[3 + k, i])
            copy.start()
            stores.append(copy)
    for copy in stores:
        copy.wait()


def solution(mesh):
    ring, parts = mesh.shape["space"], mesh.shape["tm"]

    def on_device(sep_block, own_couple, prev_couple, inner_diag):
        rows, width = sep_block.shape[1:]

        def block(kind, *lead):
            return pltpu.VMEM((*lead, rows, width), kind)

        def full(*lead):
            return pltpu.VMEM((*lead, width, width), jnp.bfloat16)

        line = pltpu.VMEM((1, width), jnp.float32)
        lines = pltpu.VMEM((ring, 1, width), jnp.float32)
        half = jnp.bfloat16
        dma = lambda count: pltpu.SemaphoreType.DMA((count,))
        cells = pltpu.VMEM((ring, rows, -(-rows // 128) * 128), half)
        taken, link = pl.pallas_call(
            functools.partial(kernel, ring, parts),
            out_shape=(
                jax.ShapeDtypeStruct((rows, width), half),
                jax.ShapeDtypeStruct((rows, width), half),
            ),
            in_specs=[pl.BlockSpec(memory_space=pl.ANY)] * 3
            + [pl.BlockSpec(memory_space=pltpu.VMEM)],
            out_specs=(pl.BlockSpec(memory_space=pltpu.VMEM),) * 2,
            scratch_shapes=[
                block(jnp.float32), full(2), block(half, 2), *[block(half)] * 10,
                block(half), block(jnp.float32), block(half), *[cells] * 6,
                line, line, line, lines, line, line, lines,
                dma(3), dma(2 * ring), dma(2 * ring), dma(4 * ring), dma(4 * ring),
                dma(ring - 1), dma(ring - 1), dma(ring - 1), dma(ring - 1),
                dma(2), dma(2), dma(5), dma(5), dma(ring), dma(ring), pltpu.SemaphoreType.REGULAR,
            ],
            compiler_params=pltpu.CompilerParams(
                collective_id=0, has_side_effects=True, vmem_limit_bytes=63 * 2**20
            ),
            cost_estimate=pl.CostEstimate(
                flops=7 * 2 * rows * width * width, bytes_accessed=10 * rows * width, transcendentals=0
            ),
        )(sep_block[0], own_couple[0], prev_couple[0], inner_diag)
        schur, link = pl.pallas_call(
            finish,
            out_shape=(
                jax.ShapeDtypeStruct((rows, width), jnp.float32),
                jax.ShapeDtypeStruct((rows, width), half),
            ),
            in_specs=[pl.BlockSpec(memory_space=pl.ANY)] * 3,
            out_specs=(pl.BlockSpec(memory_space=pl.ANY),) * 2,
            scratch_shapes=[
                block(jnp.float32), block(half), block(half), pltpu.SemaphoreType.DMA((5, 4))
            ],
            compiler_params=pltpu.CompilerParams(vmem_limit_bytes=60 * 2**20),
        )(sep_block[0], taken, link)
        return schur[None], link[None]

    placed = (P("tm", "space", None), P("tm", "space", None), P("tm", "space", None), P("tm", None))
    return jax.shard_map(
        on_device,
        mesh=mesh,
        in_specs=placed,
        out_specs=(P("tm", "space", None), P("tm", "space", None)),
        check_vma=False,
    )
```

```python
import functools

import jax
import jax.numpy as jnp
from jax import lax
from jax.experimental import pallas as pl
from jax.experimental.pallas import tpu as pltpu
from jax.sharding import PartitionSpec as P

MESH = pl.DeviceIdType.MESH
OWN, PREV = 0, 1


def kernel(
    ring, parts, sep_hbm, own_hbm, prev_hbm, diag_ref, schur_ref, link_ref,
    sep, pair, scaled, link, link_scaled, sibling, turned, fill_scaled, handed,
    passed, passed_in, last, last_in, left, left_wide, far_left,
    link_cells, form_cells, fill_cells, square_cells, final_cells, update_in,
    reciprocal, edge, edge_in, diags, edge2, edge2_in, diags2,
    load_sem, y_send, y_recv, x_send, x_recv,
    d_send, d_recv, d2_send, d2_recv, e_send, e_recv, m_send, m_recv, t_send, t_recv, go,
):
    rows, width = sep.shape
    chunk = 16
    tile = 512
    z = lax.axis_index("space")
    t = lax.axis_index("tm")
    odd = lax.rem(t, 2)
    role = lax.rem(t, 4)
    is_odd = odd == 1
    inner = jnp.logical_or(role == 1, role == 2)
    outer = jnp.logical_not(inner)
    sib = t + 1 - 2 * odd
    across = lax.rem(t + 2 * odd - 1 + parts, parts)
    before = lax.rem(t + parts - 1, parts)
    after = lax.rem(t + 1, parts)
    first, second = 1 - odd, odd

    barrier = pltpu.get_barrier_semaphore()
    for k in range(1, ring):
        pl.semaphore_signal(
            barrier, inc=1, device_id={"space": lax.rem(z + k, ring)}, device_id_type=MESH
        )
    for peer in (before, after):
        pl.semaphore_signal(barrier, inc=1, device_id={"tm": peer}, device_id_type=MESH)

    def near(d):
        return lax.rem(z + d + ring, ring)

    def row_slice(d):
        return pl.ds(pl.multiple_of(near(d) * rows, rows), rows)

    def cell_columns(j):
        return slice(j * rows, (j + 1) * rows)

    loads = [
        pltpu.make_async_copy(own_hbm, pair.at[OWN, row_slice(0)], load_sem.at[0]),
        pltpu.make_async_copy(prev_hbm, pair.at[PREV, row_slice(0)], load_sem.at[1]),
        pltpu.make_async_copy(sep_hbm, sep, load_sem.at[2]),
    ]
    for load in loads:
        load.start()
    pl.semaphore_wait(barrier, ring + 1)

    def along(src, dst, way, send_sem, recv_sem):
        return pltpu.make_async_remote_copy(
            src_ref=src, dst_ref=dst, send_sem=send_sem, recv_sem=recv_sem,
            device_id={"space": near(way)}, device_id_type=MESH,
        )

    def to_part(src, dst, peer, send_sem, recv_sem):
        return pltpu.make_async_remote_copy(
            src_ref=src, dst_ref=dst, send_sem=send_sem, recv_sem=recv_sem,
            device_id={"tm": peer}, device_id_type=MESH,
        )

    class Ring:
        def __init__(self, buf, pieces, send_sem, recv_sem):
            size = rows // pieces
            self.streams = []
            for i in range(pieces):
                long_way = 1 if i % 2 == 0 else -1
                self.streams.append((buf, i * size, size, long_way, ring // 2))
                self.streams.append((buf, i * size, size, -long_way, ring // 2 - 1))
            self.sems = send_sem, recv_sem

        def at(self, s, step):
            buf, offset, count, way, _ = self.streams[s]
            at = s * (ring // 2) + step - 1
            slot = near(-way * (step - 1))
            piece = buf.at[pl.ds(pl.multiple_of(slot * rows + offset, chunk), count)]
            return along(piece, piece, way, self.sems[0].at[at], self.sems[1].at[at])

        def start(self, begin=0, end=None):
            for s in range(len(self.streams))[begin:end]:
                self.at(s, 1).start()

        def start_from(self, source):
            for s, (buf, offset, count, way, _) in enumerate(self.streams):
                at = s * (ring // 2)
                piece = buf.at[pl.ds(pl.multiple_of(near(0) * rows + offset, chunk), count)]
                along(
                    source.at[pl.ds(offset, count)], piece, way,
                    self.sems[0].at[at], self.sems[1].at[at],
                ).start()

        def arrive(self, step):
            for s, stream in enumerate(self.streams):
                if step <= stream[4]:
                    self.at(s, step).wait_recv()
                    if step < stream[4]:
                        self.at(s, step + 1).start()

        def drain(self):
            for s, stream in enumerate(self.streams):
                for step in range(1, stream[4] + 1):
                    self.at(s, step).wait_send()

    x_all = pair.at[first]
    y_all = pair.at[second]
    ring_y = Ring(y_all, 2, y_send, y_recv)
    ring_x = Ring(x_all, 4, x_send, x_recv)

    @pl.when(is_odd)
    def _():
        ring_y.start_from(prev_hbm)

    @pl.when(jnp.logical_not(is_odd))
    def _():
        ring_y.start_from(own_hbm)

    for load in loads[:2]:
        load.wait()

    def diag_part(out, sep_factor, terms):
        out[...] = jnp.zeros_like(out)

        @pl.loop(0, rows // chunk)
        def _(i):
            at = pl.multiple_of(i * chunk, chunk)
            total = jnp.zeros((chunk, 1), jnp.float32)
            for left_rows, right_rows in terms:
                total += jnp.sum(
                    left_rows[pl.ds(at, chunk), :].astype(jnp.float32)
                    * right_rows[pl.ds(at, chunk), :].astype(jnp.float32),
                    axis=1, keepdims=True,
                )
            spot = lax.broadcasted_iota(jnp.int32, (chunk, width), 1) == (
                lax.broadcasted_iota(jnp.int32, (chunk, width), 0) + (z * rows + at)
            )
            values = sep[pl.ds(at, chunk), :] * sep_factor - total
            out[...] += jnp.sum(jnp.where(spot, values, 0.0), axis=0, keepdims=True)

    def edge_copy(edge, edge_in, peer, k):
        return to_part(edge, edge_in, peer, e_send.at[k], e_recv.at[k])

    span = 2 * rows
    my_span = pl.ds(pl.multiple_of(lax.div(z, 2) * span, span), span)

    def spread_copy(diags, s, sems):
        mine = diags.at[z, :, my_span]
        return along(mine, mine, s, sems[0].at[s - 1], sems[1].at[s - 1])

    def spread(edge, edge_in, diags, peer, k, sems):
        edge_copy(edge, edge_in, peer, k).wait()
        diags[z] = edge[...] + edge_in[...]
        for s in range(1, ring):
            spread_copy(diags, s, sems).start()

    def pivot_scale(diags, sems, out):
        for s in range(1, ring):
            spread_copy(diags, s, sems).wait_recv()
        for k in range(ring // 2):
            at = slice(k * span, (k + 1) * span)
            values = diags[2 * k, :, at] + diags[2 * k + 1, :, at]
            scale = (1.0 / jnp.maximum(values, 1.0)).astype(jnp.bfloat16)
            out[:, at] = scale.astype(jnp.float32)

    def scale_rows(source, factors, out):
        @pl.loop(0, rows // chunk)
        def _(i):
            at = pl.ds(pl.multiple_of(i * chunk, chunk), chunk)
            out[at, :] = (source[at, :].astype(jnp.float32) * factors).astype(jnp.bfloat16)

    def dot(left_rows, right_rows):
        return lax.dot_general(
            left_rows[...], right_rows[...], (((1,), (1,)), ((), ())),
            preferred_element_type=jnp.float32,
        )

    def times(left_rows, matrix, take):
        @pl.loop(0, width // tile)
        def _(j):
            at = pl.ds(pl.multiple_of(j * tile, tile), tile)
            take(at, jnp.dot(left_rows[...], matrix[:, at], preferred_element_type=jnp.float32))

    def times_turned(left_rows, matrix, take):
        @pl.loop(0, width // tile)
        def _(j):
            at = pl.ds(pl.multiple_of(j * tile, tile), tile)
            take(at, dot(left_rows, matrix.at[at]))

    def scaled_into(out, factors):
        def take(at, value):
            out[:, at] = (value * factors[:, at]).astype(jnp.bfloat16)

        return take

    cell = slice(0, rows)

    def put(cells, d, value):
        cells[near(d), :, cell] = value.astype(jnp.bfloat16)

    def x_rows(d):
        return x_all.at[row_slice(d)]

    def y_rows(d):
        return y_all.at[row_slice(d)]

    reach = {0: (0,), 4: (ring // 2,)}
    for step in range(1, ring // 2):
        reach[step] = (-step, step)

    reciprocal[...] = 1.0 / diag_ref[...]
    x_scaled, y_scaled = scaled.at[0], scaled.at[1]
    scale_rows(y_rows(0), reciprocal[...], y_scaled)
    scale_rows(x_rows(0), reciprocal[...], x_scaled)
    loads[2].wait()
    diag_part(edge, (1 - odd).astype(jnp.float32), [(y_scaled, y_rows(0))])
    edge_copy(edge, edge_in, sib, 0).start()
    spread(edge, edge_in, diags, sib, 0, (d_send, d_recv))

    sign = jnp.where(t == 0, 0.0, -1.0)

    def link_and_form(step):
        for d in reach[step]:
            put(link_cells, d, dot(x_scaled, y_rows(d)) * sign)
            put(form_cells, d, dot(y_scaled, y_rows(d)))

    link_and_form(0)
    for step in (1, 2, 3):
        ring_y.arrive(step)
        if step == 3:

            @pl.when(inner)
            def _():
                ring_x.start(0, 2)

        link_and_form(step)
    ring_y.arrive(4)

    @pl.when(inner)
    def _():
        ring_x.start(2)

    link_and_form(4)
    for j in range(ring):
        link[:, cell_columns(j)] = link_cells[j, :, cell]
    scale1 = edge
    pivot_scale(diags, (d_send, d_recv), scale1)
    scale_rows(link, scale1[...], link_scaled)

    hand_link = to_part(link_scaled, sibling, sib, m_send.at[0], m_recv.at[0])
    hand_back = to_part(passed, passed_in, sib, m_send.at[1], m_recv.at[1])
    hand_last = to_part(last, last_in, sib, m_send.at[2], m_recv.at[2])
    hand_fill = to_part(fill_scaled, handed, after, m_send.at[3], m_recv.at[3])
    send_form = to_part(form_cells, update_in, before, m_send.at[4], m_recv.at[4])
    send_square = to_part(square_cells, update_in, before, m_send.at[4], m_recv.at[4])

    @pl.when(outer)
    def _():
        hand_link.start()

    @pl.when(is_odd)
    def _():
        send_form.start()

    def take_left(at, value):
        left_wide[:, at] = x_scaled[:, at].astype(jnp.float32) - value * reciprocal[:, at]

    def round_left():
        left[...] = left_wide[...].astype(jnp.bfloat16)

    def square_cell(step):
        for d in reach[step]:
            put(square_cells, d, dot(left, x_rows(d)))

    def even_result():
        send_form.wait_recv()
        for j in range(ring):
            at = cell_columns(j)
            taken = form_cells[j, :, cell].astype(jnp.float32)
            taken += update_in[j, :, cell].astype(jnp.float32)
            schur_ref[:, at] = taken.astype(jnp.bfloat16)
        link_ref[...] = link[...]

    @pl.when(inner)
    def _():
        diag_part(
            edge2, odd.astype(jnp.float32), [(x_scaled, x_rows(0)), (link_scaled, link)]
        )
        edge_copy(edge2, edge2_in, across, 1).start()
        times(link_scaled, y_all, take_left)
        round_left()
        ring_x.arrive(1)
        hand_link.wait_recv()
        times(sibling, y_all, scaled_into(turned, reciprocal))
        spread(edge2, edge2_in, diags2, across, 1, (d2_send, d2_recv))

        def fill_cell(step):
            for d in reach[step]:
                put(fill_cells, d, dot(turned, x_rows(d)))

        fill_cell(0)
        fill_cell(1)
        ring_x.arrive(2)
        fill_cell(2)
        square_cell(0)
        square_cell(1)
        ring_x.arrive(3)
        pl.semaphore_signal(go, inc=1, device_id={"tm": sib}, device_id_type=MESH)
        fill_cell(3)
        pivot_scale(diags2, (d2_send, d2_recv), edge2)
        ring_x.arrive(4)
        fill_cell(4)
        for j in range(ring):
            turned[:, cell_columns(j)] = fill_cells[j, :, cell]
        scale_rows(turned, edge2[...], fill_scaled)

        @pl.when(role == 1)
        def _():
            hand_fill.start()

        times(fill_scaled, x_all, scaled_into(sibling, reciprocal))
        times_turned(sibling, y_all, scaled_into(passed, scale1))
        hand_back.start()
        square_cell(2)
        square_cell(3)
        square_cell(4)

        @pl.when(role == 2)
        def _():
            send_square.start()
            hand_fill.wait_recv()
            times(handed, x_all, scaled_into(sibling, reciprocal))
            times_turned(sibling, y_all, scaled_into(last, scale1))
            hand_last.start()
            even_result()

        @pl.when(role == 1)
        def _():
            link_ref[...] = turned[...]
            send_square.wait_recv()
            for j in range(ring):
                at = cell_columns(j)
                taken = square_cells[j, :, cell].astype(jnp.float32)
                taken += update_in[j, :, cell].astype(jnp.float32)
                schur_ref[:, at] = taken.astype(jnp.bfloat16)

    order = [d for step in range(ring // 2 + 1) for d in reach[step]]

    def send_cell(d):
        i = order.index(d)
        cells = square_cells.at[near(d)]
        return to_part(cells, update_in.at[near(d)], before, t_send.at[i], t_recv.at[i])

    @pl.when(outer)
    def _():
        times(link_scaled, y_all, take_left)

        @pl.when(role == 0)
        def _():
            even_result()

        pl.semaphore_wait(go, 1)
        ring_x.start()

        def outer_cells(step):
            square_cell(step)

            @pl.when(role == 0)
            def _():
                for d in reach[step]:
                    send_cell(d).start()

        def final_cell(step):
            for d in reach[step]:
                put(final_cells, d, dot(far_left, x_rows(d)))

        ring_x.arrive(1)
        ring_x.arrive(2)
        hand_back.wait_recv()

        def take_more(at, value):
            left_wide[:, at] -= value * reciprocal[:, at]

        times(passed_in, y_all, take_more)
        round_left()
        outer_cells(0)
        outer_cells(1)
        outer_cells(2)
        ring_x.arrive(3)
        outer_cells(3)

        @pl.when(role == 3)
        def _():
            hand_last.wait_recv()
            times(last_in, y_all, scaled_into(far_left, reciprocal))
            for step in range(4):
                final_cell(step)

        ring_x.arrive(4)
        outer_cells(4)

        @pl.when(role == 3)
        def _():
            final_cell(4)
            for j in range(ring):
                at = cell_columns(j)
                schur_ref[:, at] = square_cells[j, :, cell]
                link_ref[:, at] = final_cells[j, :, cell]
            for d in order:
                send_cell(d).wait_recv()

            @pl.when(t != parts - 1)
            def _():
                for j in range(ring):
                    at = cell_columns(j)
                    taken = square_cells[j, :, cell].astype(jnp.float32)
                    taken += update_in[j, :, cell].astype(jnp.float32)
                    schur_ref[:, at] = taken.astype(jnp.bfloat16)

    ring_y.drain()
    ring_x.drain()
    for s in range(1, ring):
        spread_copy(diags, s, (d_send, d_recv)).wait_send()

    @pl.when(inner)
    def _():
        hand_back.wait_send()
        for s in range(1, ring):
            spread_copy(diags2, s, (d2_send, d2_recv)).wait_send()

    @pl.when(outer)
    def _():
        hand_link.wait_send()

    @pl.when(is_odd)
    def _():
        send_form.wait_send()

    @pl.when(role == 0)
    def _():
        for d in order:
            send_cell(d).wait_send()

    @pl.when(role == 1)
    def _():
        hand_fill.wait_send()

    @pl.when(role == 2)
    def _():
        send_square.wait_send()
        hand_last.wait_send()


def finish(sep_in, taken_in, link_in, schur_out, link_out, sep, taken, link, sems):
    count = 6
    step = sep_in.shape[0] // count
    slabs = [pl.ds(i * step, step) for i in range(count)]
    loads, stores = [], []
    for i, at in enumerate(slabs):
        for k, (src, dst) in enumerate(((sep_in, sep), (taken_in, taken), (link_in, link))):
            copy = pltpu.make_async_copy(src.at[at], dst.at[at], sems.at[k, i])
            copy.start()
            loads.append(copy)
    for i, at in enumerate(slabs):
        for k in range(3):
            loads[3 * i + k].wait()
        sep[at, :] -= taken[at, :].astype(jnp.float32)
        for k, (src, dst) in enumerate(((sep, schur_out), (link, link_out))):
            copy = pltpu.make_async_copy(src.at[at], dst.at[at], sems.at[3 + k, i])
            copy.start()
            stores.append(copy)
    for copy in stores:
        copy.wait()


def solution(mesh):
    ring, parts = mesh.shape["space"], mesh.shape["tm"]

    def on_device(sep_block, own_couple, prev_couple, inner_diag):
        rows, width = sep_block.shape[1:]

        def block(kind, *lead):
            return pltpu.VMEM((*lead, rows, width), kind)

        def full(*lead):
            return pltpu.VMEM((*lead, width, width), jnp.bfloat16)

        line = pltpu.VMEM((1, width), jnp.float32)
        lines = pltpu.VMEM((ring, 1, width), jnp.float32)
        half = jnp.bfloat16
        dma = lambda count: pltpu.SemaphoreType.DMA((count,))
        cells = pltpu.VMEM((ring, rows, -(-rows // 128) * 128), half)
        taken, link = pl.pallas_call(
            functools.partial(kernel, ring, parts),
            out_shape=(
                jax.ShapeDtypeStruct((rows, width), half),
                jax.ShapeDtypeStruct((rows, width), half),
            ),
            in_specs=[pl.BlockSpec(memory_space=pl.ANY)] * 3
            + [pl.BlockSpec(memory_space=pltpu.VMEM)],
            out_specs=(pl.BlockSpec(memory_space=pltpu.VMEM),) * 2,
            scratch_shapes=[
                block(jnp.float32), full(2), block(half, 2), *[block(half)] * 10,
                block(half), block(jnp.float32), block(half), *[cells] * 6,
                line, line, line, lines, line, line, lines,
                dma(3), dma(2 * ring), dma(2 * ring), dma(4 * ring), dma(4 * ring),
                dma(ring - 1), dma(ring - 1), dma(ring - 1), dma(ring - 1),
                dma(2), dma(2), dma(5), dma(5), dma(ring), dma(ring), pltpu.SemaphoreType.REGULAR,
            ],
            compiler_params=pltpu.CompilerParams(
                collective_id=0, has_side_effects=True, vmem_limit_bytes=63 * 2**20
            ),
            cost_estimate=pl.CostEstimate(
                flops=7 * 2 * rows * width * width, bytes_accessed=10 * rows * width, transcendentals=0
            ),
        )(sep_block[0], own_couple[0], prev_couple[0], inner_diag)
        schur, link = pl.pallas_call(
            finish,
            out_shape=(
                jax.ShapeDtypeStruct((rows, width), jnp.float32),
                jax.ShapeDtypeStruct((rows, width), half),
            ),
            in_specs=[pl.BlockSpec(memory_space=pl.ANY)] * 3,
            out_specs=(pl.BlockSpec(memory_space=pl.ANY),) * 2,
            scratch_shapes=[
                block(jnp.float32), block(half), block(half), pltpu.SemaphoreType.DMA((5, 6))
            ],
            compiler_params=pltpu.CompilerParams(vmem_limit_bytes=60 * 2**20),
        )(sep_block[0], taken, link)
        return schur[None], link[None]

    placed = (P("tm", "space", None), P("tm", "space", None), P("tm", "space", None), P("tm", None))
    return jax.shard_map(
        on_device,
        mesh=mesh,
        in_specs=placed,
        out_specs=(P("tm", "space", None), P("tm", "space", None)),
        check_vma=False,
    )
```

```python
import functools

import jax
import jax.numpy as jnp
from jax import lax
from jax.experimental import pallas as pl
from jax.experimental.pallas import tpu as pltpu
from jax.sharding import PartitionSpec as P

MESH = pl.DeviceIdType.MESH
OWN, PREV = 0, 1


def kernel(
    ring, parts, sep_hbm, own_hbm, prev_hbm, diag_ref, schur_ref, link_ref,
    sep, pair, scaled, link, link_scaled, sibling, turned, fill_scaled, handed,
    passed, passed_in, last, last_in, left, left_wide, far_left,
    link_cells, form_cells, fill_cells, square_cells, final_cells, update_in,
    reciprocal, edge, edge_in, diags, edge2, edge2_in, diags2,
    load_sem, y_send, y_recv, x_send, x_recv,
    d_send, d_recv, d2_send, d2_recv, e_send, e_recv, m_send, m_recv, t_send, t_recv, go,
):
    rows, width = sep.shape
    chunk = 16
    tile = 512
    z = lax.axis_index("space")
    t = lax.axis_index("tm")
    odd = lax.rem(t, 2)
    role = lax.rem(t, 4)
    is_odd = odd == 1
    inner = jnp.logical_or(role == 1, role == 2)
    outer = jnp.logical_not(inner)
    sib = t + 1 - 2 * odd
    across = lax.rem(t + 2 * odd - 1 + parts, parts)
    before = lax.rem(t + parts - 1, parts)
    after = lax.rem(t + 1, parts)
    first, second = 1 - odd, odd

    barrier = pltpu.get_barrier_semaphore()
    for k in range(1, ring):
        pl.semaphore_signal(
            barrier, inc=1, device_id={"space": lax.rem(z + k, ring)}, device_id_type=MESH
        )
    for peer in (before, after):
        pl.semaphore_signal(barrier, inc=1, device_id={"tm": peer}, device_id_type=MESH)

    def near(d):
        return lax.rem(z + d + ring, ring)

    def row_slice(d):
        return pl.ds(pl.multiple_of(near(d) * rows, rows), rows)

    def cell_columns(j):
        return slice(j * rows, (j + 1) * rows)

    loads = [
        pltpu.make_async_copy(own_hbm, pair.at[OWN, row_slice(0)], load_sem.at[0]),
        pltpu.make_async_copy(prev_hbm, pair.at[PREV, row_slice(0)], load_sem.at[1]),
        pltpu.make_async_copy(sep_hbm, sep, load_sem.at[2]),
    ]
    for load in loads:
        load.start()
    for load in loads:
        load.wait()
    pl.semaphore_wait(barrier, ring + 1)

    def along(src, dst, way, send_sem, recv_sem):
        return pltpu.make_async_remote_copy(
            src_ref=src, dst_ref=dst, send_sem=send_sem, recv_sem=recv_sem,
            device_id={"space": near(way)}, device_id_type=MESH,
        )

    def to_part(src, dst, peer, send_sem, recv_sem):
        return pltpu.make_async_remote_copy(
            src_ref=src, dst_ref=dst, send_sem=send_sem, recv_sem=recv_sem,
            device_id={"tm": peer}, device_id_type=MESH,
        )

    class Ring:
        def __init__(self, buf, pieces, send_sem, recv_sem):
            size = rows // pieces
            self.streams = []
            for i in range(pieces):
                long_way = 1 if i % 2 == 0 else -1
                self.streams.append((buf, i * size, size, long_way, ring // 2))
                self.streams.append((buf, i * size, size, -long_way, ring // 2 - 1))
            self.sems = send_sem, recv_sem

        def at(self, s, step):
            buf, offset, count, way, _ = self.streams[s]
            at = s * (ring // 2) + step - 1
            slot = near(-way * (step - 1))
            piece = buf.at[pl.ds(pl.multiple_of(slot * rows + offset, chunk), count)]
            return along(piece, piece, way, self.sems[0].at[at], self.sems[1].at[at])

        def start(self, begin=0, end=None):
            for s in range(len(self.streams))[begin:end]:
                self.at(s, 1).start()

        def arrive(self, step, begin=0, end=None):
            for s, stream in list(enumerate(self.streams))[begin:end]:
                if step <= stream[4]:
                    self.at(s, step).wait_recv()
                    if step < stream[4]:
                        self.at(s, step + 1).start()

        def drain(self):
            for s, stream in enumerate(self.streams):
                for step in range(1, stream[4] + 1):
                    self.at(s, step).wait_send()

    x_all = pair.at[first]
    y_all = pair.at[second]
    ring_y = Ring(y_all, 2, y_send, y_recv)
    ring_x = Ring(x_all, 4, x_send, x_recv)
    ring_y.start()

    def diag_part(out, sep_factor, terms):
        out[...] = jnp.zeros_like(out)

        @pl.loop(0, rows // chunk)
        def _(i):
            at = pl.multiple_of(i * chunk, chunk)
            total = jnp.zeros((chunk, 1), jnp.float32)
            for left_rows, right_rows in terms:
                total += jnp.sum(
                    left_rows[pl.ds(at, chunk), :].astype(jnp.float32)
                    * right_rows[pl.ds(at, chunk), :].astype(jnp.float32),
                    axis=1, keepdims=True,
                )
            spot = lax.broadcasted_iota(jnp.int32, (chunk, width), 1) == (
                lax.broadcasted_iota(jnp.int32, (chunk, width), 0) + (z * rows + at)
            )
            values = sep[pl.ds(at, chunk), :] * sep_factor - total
            out[...] += jnp.sum(jnp.where(spot, values, 0.0), axis=0, keepdims=True)

    def edge_copy(edge, edge_in, peer, k):
        return to_part(edge, edge_in, peer, e_send.at[k], e_recv.at[k])

    span = 2 * rows
    my_span = pl.ds(pl.multiple_of(lax.div(z, 2) * span, span), span)

    def spread_copy(diags, s, sems):
        mine = diags.at[z, :, my_span]
        return along(mine, mine, s, sems[0].at[s - 1], sems[1].at[s - 1])

    def spread(edge, edge_in, diags, peer, k, sems):
        edge_copy(edge, edge_in, peer, k).wait()
        diags[z] = edge[...] + edge_in[...]
        for s in range(1, ring):
            spread_copy(diags, s, sems).start()

    def pivot_scale(diags, sems, out):
        for s in range(1, ring):
            spread_copy(diags, s, sems).wait_recv()
        for k in range(ring // 2):
            at = slice(k * span, (k + 1) * span)
            values = diags[2 * k, :, at] + diags[2 * k + 1, :, at]
            scale = (1.0 / jnp.maximum(values, 1.0)).astype(jnp.bfloat16)
            out[:, at] = scale.astype(jnp.float32)

    def scale_rows(source, factors, out):
        @pl.loop(0, rows // chunk)
        def _(i):
            at = pl.ds(pl.multiple_of(i * chunk, chunk), chunk)
            out[at, :] = (source[at, :].astype(jnp.float32) * factors).astype(jnp.bfloat16)

    def dot(left_rows, right_rows):
        return lax.dot_general(
            left_rows[...], right_rows[...], (((1,), (1,)), ((), ())),
            preferred_element_type=jnp.float32,
        )

    def times(left_rows, matrix, take):
        @pl.loop(0, width // tile)
        def _(j):
            at = pl.ds(pl.multiple_of(j * tile, tile), tile)
            take(at, jnp.dot(left_rows[...], matrix[:, at], preferred_element_type=jnp.float32))

    def times_turned(left_rows, matrix, take):
        @pl.loop(0, width // tile)
        def _(j):
            at = pl.ds(pl.multiple_of(j * tile, tile), tile)
            take(at, dot(left_rows, matrix.at[at]))

    def scaled_into(out, factors):
        def take(at, value):
            out[:, at] = (value * factors[:, at]).astype(jnp.bfloat16)

        return take

    cell = slice(0, rows)

    def put(cells, d, value):
        cells[near(d), :, cell] = value.astype(jnp.bfloat16)

    def x_rows(d):
        return x_all.at[row_slice(d)]

    def y_rows(d):
        return y_all.at[row_slice(d)]

    reach = {0: (0,), 4: (ring // 2,)}
    for step in range(1, ring // 2):
        reach[step] = (-step, step)

    reciprocal[...] = 1.0 / diag_ref[...]
    x_scaled, y_scaled = scaled.at[0], scaled.at[1]
    scale_rows(y_rows(0), reciprocal[...], y_scaled)
    scale_rows(x_rows(0), reciprocal[...], x_scaled)
    diag_part(edge, (1 - odd).astype(jnp.float32), [(y_scaled, y_rows(0))])
    edge_copy(edge, edge_in, sib, 0).start()
    spread(edge, edge_in, diags, sib, 0, (d_send, d_recv))

    sign = jnp.where(t == 0, 0.0, -1.0)

    def link_and_form(step):
        for d in reach[step]:
            put(link_cells, d, dot(x_scaled, y_rows(d)) * sign)
            put(form_cells, d, dot(y_scaled, y_rows(d)))

    link_and_form(0)
    for step in (1, 2, 3):
        ring_y.arrive(step)
        if step == 3:

            @pl.when(inner)
            def _():
                ring_x.start(0, 2)

        link_and_form(step)
    ring_y.arrive(4)

    @pl.when(inner)
    def _():
        ring_x.start(2)

    link_and_form(4)
    for j in range(ring):
        link[:, cell_columns(j)] = link_cells[j, :, cell]
    scale1 = edge
    pivot_scale(diags, (d_send, d_recv), scale1)
    scale_rows(link, scale1[...], link_scaled)

    hand_link = to_part(link_scaled, sibling, sib, m_send.at[0], m_recv.at[0])
    hand_back = to_part(passed, passed_in, sib, m_send.at[1], m_recv.at[1])
    hand_last = to_part(last, last_in, sib, m_send.at[2], m_recv.at[2])
    hand_fill = to_part(fill_scaled, handed, after, m_send.at[3], m_recv.at[3])
    send_form = to_part(form_cells, update_in, before, m_send.at[4], m_recv.at[4])
    send_square = to_part(square_cells, update_in, before, m_send.at[4], m_recv.at[4])

    @pl.when(outer)
    def _():
        hand_link.start()

    @pl.when(is_odd)
    def _():
        send_form.start()

    def take_left(at, value):
        left_wide[:, at] = x_scaled[:, at].astype(jnp.float32) - value * reciprocal[:, at]

    def round_left():
        left[...] = left_wide[...].astype(jnp.bfloat16)

    def square_cell(step):
        for d in reach[step]:
            put(square_cells, d, dot(left, x_rows(d)))

    def even_result():
        send_form.wait_recv()
        for j in range(ring):
            at = cell_columns(j)
            taken = form_cells[j, :, cell].astype(jnp.float32)
            taken += update_in[j, :, cell].astype(jnp.float32)
            schur_ref[:, at] = taken.astype(jnp.bfloat16)
        link_ref[...] = link[...]

    @pl.when(inner)
    def _():
        diag_part(
            edge2, odd.astype(jnp.float32), [(x_scaled, x_rows(0)), (link_scaled, link)]
        )
        edge_copy(edge2, edge2_in, across, 1).start()
        times(link_scaled, y_all, take_left)
        round_left()
        ring_x.arrive(1)
        hand_link.wait_recv()
        times(sibling, y_all, scaled_into(turned, reciprocal))
        spread(edge2, edge2_in, diags2, across, 1, (d2_send, d2_recv))

        def fill_cell(step):
            for d in reach[step]:
                put(fill_cells, d, dot(turned, x_rows(d)))

        fill_cell(0)
        fill_cell(1)
        ring_x.arrive(2)
        fill_cell(2)
        square_cell(0)
        square_cell(1)
        ring_x.arrive(3)
        pl.semaphore_signal(go, inc=1, device_id={"tm": sib}, device_id_type=MESH)
        fill_cell(3)
        pivot_scale(diags2, (d2_send, d2_recv), edge2)
        ring_x.arrive(4)
        fill_cell(4)
        for j in range(ring):
            turned[:, cell_columns(j)] = fill_cells[j, :, cell]
        scale_rows(turned, edge2[...], fill_scaled)

        @pl.when(role == 1)
        def _():
            hand_fill.start()

        times(fill_scaled, x_all, scaled_into(sibling, reciprocal))
        times_turned(sibling, y_all, scaled_into(passed, scale1))
        hand_back.start()
        square_cell(2)
        square_cell(3)
        square_cell(4)

        @pl.when(role == 2)
        def _():
            send_square.start()
            hand_fill.wait_recv()
            times(handed, x_all, scaled_into(sibling, reciprocal))
            times_turned(sibling, y_all, scaled_into(last, scale1))
            hand_last.start()
            even_result()

        @pl.when(role == 1)
        def _():
            link_ref[...] = turned[...]
            send_square.wait_recv()
            for j in range(ring):
                at = cell_columns(j)
                taken = square_cells[j, :, cell].astype(jnp.float32)
                taken += update_in[j, :, cell].astype(jnp.float32)
                schur_ref[:, at] = taken.astype(jnp.bfloat16)

    order = [d for step in range(ring // 2 + 1) for d in reach[step]]

    def send_cell(d):
        i = order.index(d)
        cells = square_cells.at[near(d)]
        return to_part(cells, update_in.at[near(d)], before, t_send.at[i], t_recv.at[i])

    @pl.when(outer)
    def _():
        ring_x.start(0, 2)
        times(link_scaled, y_all, take_left)

        @pl.when(role == 0)
        def _():
            even_result()

        ring_x.arrive(1, 0, 2)
        pl.semaphore_wait(go, 1)
        ring_x.start(2)

        def outer_cells(step):
            square_cell(step)

            @pl.when(role == 0)
            def _():
                for d in reach[step]:
                    send_cell(d).start()

        def final_cell(step):
            for d in reach[step]:
                put(final_cells, d, dot(far_left, x_rows(d)))

        ring_x.arrive(1, 2)
        ring_x.arrive(2)
        hand_back.wait_recv()

        def take_more(at, value):
            left_wide[:, at] -= value * reciprocal[:, at]

        times(passed_in, y_all, take_more)
        round_left()
        outer_cells(0)
        outer_cells(1)
        outer_cells(2)
        ring_x.arrive(3)
        outer_cells(3)

        @pl.when(role == 3)
        def _():
            hand_last.wait_recv()
            times(last_in, y_all, scaled_into(far_left, reciprocal))
            for step in range(4):
                final_cell(step)

        ring_x.arrive(4)
        outer_cells(4)

        @pl.when(role == 3)
        def _():
            final_cell(4)
            for j in range(ring):
                at = cell_columns(j)
                schur_ref[:, at] = square_cells[j, :, cell]
                link_ref[:, at] = final_cells[j, :, cell]
            for d in order:
                send_cell(d).wait_recv()

            @pl.when(t != parts - 1)
            def _():
                for j in range(ring):
                    at = cell_columns(j)
                    taken = square_cells[j, :, cell].astype(jnp.float32)
                    taken += update_in[j, :, cell].astype(jnp.float32)
                    schur_ref[:, at] = taken.astype(jnp.bfloat16)

    ring_y.drain()
    ring_x.drain()
    for s in range(1, ring):
        spread_copy(diags, s, (d_send, d_recv)).wait_send()

    @pl.when(inner)
    def _():
        hand_back.wait_send()
        for s in range(1, ring):
            spread_copy(diags2, s, (d2_send, d2_recv)).wait_send()

    @pl.when(outer)
    def _():
        hand_link.wait_send()

    @pl.when(is_odd)
    def _():
        send_form.wait_send()

    @pl.when(role == 0)
    def _():
        for d in order:
            send_cell(d).wait_send()

    @pl.when(role == 1)
    def _():
        hand_fill.wait_send()

    @pl.when(role == 2)
    def _():
        send_square.wait_send()
        hand_last.wait_send()


def finish(sep_in, taken_in, link_in, schur_out, link_out, sep, taken, link, sems):
    count = 4
    step = sep_in.shape[0] // count
    slabs = [pl.ds(i * step, step) for i in range(count)]
    loads, stores = [], []
    for i, at in enumerate(slabs):
        for k, (src, dst) in enumerate(((sep_in, sep), (taken_in, taken), (link_in, link))):
            copy = pltpu.make_async_copy(src.at[at], dst.at[at], sems.at[k, i])
            copy.start()
            loads.append(copy)
    for i, at in enumerate(slabs):
        for k in range(3):
            loads[3 * i + k].wait()
        sep[at, :] -= taken[at, :].astype(jnp.float32)
        for k, (src, dst) in enumerate(((sep, schur_out), (link, link_out))):
            copy = pltpu.make_async_copy(src.at[at], dst.at[at], sems.at[3 + k, i])
            copy.start()
            stores.append(copy)
    for copy in stores:
        copy.wait()


def solution(mesh):
    ring, parts = mesh.shape["space"], mesh.shape["tm"]

    def on_device(sep_block, own_couple, prev_couple, inner_diag):
        rows, width = sep_block.shape[1:]

        def block(kind, *lead):
            return pltpu.VMEM((*lead, rows, width), kind)

        def full(*lead):
            return pltpu.VMEM((*lead, width, width), jnp.bfloat16)

        line = pltpu.VMEM((1, width), jnp.float32)
        lines = pltpu.VMEM((ring, 1, width), jnp.float32)
        half = jnp.bfloat16
        dma = lambda count: pltpu.SemaphoreType.DMA((count,))
        cells = pltpu.VMEM((ring, rows, -(-rows // 128) * 128), half)
        taken, link = pl.pallas_call(
            functools.partial(kernel, ring, parts),
            out_shape=(
                jax.ShapeDtypeStruct((rows, width), half),
                jax.ShapeDtypeStruct((rows, width), half),
            ),
            in_specs=[pl.BlockSpec(memory_space=pl.ANY)] * 3
            + [pl.BlockSpec(memory_space=pltpu.VMEM)],
            out_specs=(pl.BlockSpec(memory_space=pltpu.VMEM),) * 2,
            scratch_shapes=[
                block(jnp.float32), full(2), block(half, 2), *[block(half)] * 10,
                block(half), block(jnp.float32), block(half), *[cells] * 6,
                line, line, line, lines, line, line, lines,
                dma(3), dma(2 * ring), dma(2 * ring), dma(4 * ring), dma(4 * ring),
                dma(ring - 1), dma(ring - 1), dma(ring - 1), dma(ring - 1),
                dma(2), dma(2), dma(5), dma(5), dma(ring), dma(ring), pltpu.SemaphoreType.REGULAR,
            ],
            compiler_params=pltpu.CompilerParams(
                collective_id=0, has_side_effects=True, vmem_limit_bytes=63 * 2**20
            ),
            cost_estimate=pl.CostEstimate(
                flops=7 * 2 * rows * width * width, bytes_accessed=10 * rows * width, transcendentals=0
            ),
        )(sep_block[0], own_couple[0], prev_couple[0], inner_diag)
        schur, link = pl.pallas_call(
            finish,
            out_shape=(
                jax.ShapeDtypeStruct((rows, width), jnp.float32),
                jax.ShapeDtypeStruct((rows, width), half),
            ),
            in_specs=[pl.BlockSpec(memory_space=pl.ANY)] * 3,
            out_specs=(pl.BlockSpec(memory_space=pl.ANY),) * 2,
            scratch_shapes=[
                block(jnp.float32), block(half), block(half), pltpu.SemaphoreType.DMA((5, 4))
            ],
            compiler_params=pltpu.CompilerParams(vmem_limit_bytes=60 * 2**20),
        )(sep_block[0], taken, link)
        return schur[None], link[None]

    placed = (P("tm", "space", None), P("tm", "space", None), P("tm", "space", None), P("tm", None))
    return jax.shard_map(
        on_device,
        mesh=mesh,
        in_specs=placed,
        out_specs=(P("tm", "space", None), P("tm", "space", None)),
        check_vma=False,
    )
```
